32 devices in a mesh: sta: 16 (over z, y, x), stk: 2 (over core).
Axes of the slice: x: 2, y: 2, z: 4, core: 2. Of those that a mesh axis runs over, the one named last changes fastest.
Arguments:
- spectra: float32 [2, 64, 2, 2048], P('stk', 'sta')
- partner_masks: int32 [4], replicated, may hold values from 1 to 15, as said below
Outputs:
- correlations: float32 [256, 4, 2400], P(('sta', 'stk'))
The draws below stay inside these ranges and needn't reach their ends.
Inputs may be any that keep to these rules, and one draw needn't show every extreme that they name: `partner_masks`: each round's block pairing is b with b XOR mask; every bit below log2 of the number of station blocks is set in some round's mask.
All inputs are finite; a program needn't handle non-finite values.
Results may differ from the reference program's by a relative error of at most 0.0037.
Values may be sent and summed in bfloat16 or wider, within the bound.
A program may use at most 64 MiB of HBM per device.

```python
import jax
import jax.numpy as jnp
from jax import lax

SB = 4
ROUNDS = 4
FB = 2048
NFFT = 8192
MAXLAG = 1200
STATIONS = 64
WINDOWS = 2
N_STA = 16


def draw_spectra(key, part):
    first_key, second_key, third_key = jax.random.split(key, 3)
    shape_full = (WINDOWS, STATIONS, 2, FB)
    noise = jax.random.normal(first_key, shape_full, jnp.float32)
    log_bins = jax.random.uniform(second_key, (WINDOWS, STATIONS, 1, FB), jnp.float32, -2.3, 2.3)
    log_station = jax.random.uniform(third_key, (1, STATIONS, 1, 1), jnp.float32, -1.15, 1.15)
    return noise * jnp.exp(log_bins + log_station)


def draw_partner_masks(key, part):
    raw_masks = jax.random.randint(key, (ROUNDS,), 1, N_STA, jnp.int32)
    covered = jnp.bitwise_or(raw_masks[0], jnp.bitwise_xor(raw_masks[1], N_STA - 1))
    return raw_masks.at[0].set(covered)


def setup_inputs(seed: int = 0) -> dict:
    key_of = jax.random.split(jax.random.key(seed), 3)
    return {
        "spectra": draw_spectra(jax.random.fold_in(key_of[2], 71), 0),
        "partner_masks": draw_partner_masks(jax.random.fold_in(key_of[2], 71), 0),
    }


def reference(spectra, partner_masks):
    power_spec = spectra[:, :, 0] ** 2 + spectra[:, :, 1] ** 2
    water_base = lax.optimization_barrier(jnp.mean(power_spec, axis=-1, keepdims=True))
    denom = jnp.sqrt(power_spec + 0.05 * (water_base + 1e-06))
    whitened = (spectra / denom[:, :, None, :]).astype(jnp.bfloat16).astype(jnp.float32)
    blocks = whitened.reshape(WINDOWS, N_STA, SB, 2, FB)
    normalizer = 1.0 / jnp.sqrt(jnp.float32(WINDOWS * FB))

    def one_round(round_mask):
        block_ids = jnp.arange(N_STA, dtype=jnp.int32)
        partner_ids = jnp.bitwise_xor(block_ids, round_mask.astype(jnp.int32))
        partner_blocks = jnp.take(blocks, partner_ids, axis=1)
        own_re = blocks[:, :, :, 0]
        own_im = blocks[:, :, :, 1]
        far_re = partner_blocks[:, :, :, 0]
        far_im = partner_blocks[:, :, :, 1]
        real_part = jnp.einsum('wbik,wbjk->bijk', own_re, far_re) + jnp.einsum('wbik,wbjk->bijk', own_im, far_im)
        imag_part = jnp.einsum('wbik,wbjk->bijk', own_im, far_re) - jnp.einsum('wbik,wbjk->bijk', own_re, far_im)
        spectrum = lax.complex(real_part, imag_part)
        padded = jnp.pad(spectrum, ((0, 0), (0, 0), (0, 0), (0, NFFT // 2 + 1 - FB)))
        series = jnp.fft.irfft(padded, n=NFFT, axis=-1) * NFFT * normalizer
        lagged = jnp.concatenate([series[..., NFFT - MAXLAG:], series[..., :MAXLAG]], axis=-1)
        return lagged.reshape(N_STA * SB * SB, 2 * MAXLAG)
    per_round = lax.map(one_round, partner_masks)
    return jnp.transpose(per_round, (1, 0, 2))
```

```python
import functools
import math

import jax
import jax.numpy as jnp
import ml_dtypes
import numpy as np
from jax import lax
from jax.experimental import pallas as pl
from jax.experimental.pallas import tpu as pltpu
from jax.sharding import PartitionSpec as P

NFFT = 8192
MAXLAG = 1200
LANES = 128
FINE = NFFT // LANES
GROUPS = -(-2 * MAXLAG // LANES)
GROUP_ROWS = -(-GROUPS // 8) * 8
MESH = pl.DeviceIdType.MESH
VMEM = pl.BlockSpec(memory_space=pltpu.VMEM)


def routes(count):
    plan = []
    by_level = sorted(range(1, count), key=lambda d: (bin(d).count("1"), d))
    for d in by_level:
        high = d & ~3
        low = d & 3
        if low == 0:
            hop = high & -high
        elif low == 3:
            hop = 1 if bin(high).count("1") % 2 == 0 else 2
        else:
            hop = low
        plan.append((d, d ^ hop, hop))
    return plan


def gather_kernel(
    n_sta, n_stk, x_ref, mask_ref, own_ref, far_ref, stage, slots, send_sem, recv_sem,
    own_send, own_recv, far_send, far_recv,
):
    sta = lax.axis_index("sta")
    stk = lax.axis_index("stk")
    plan = routes(n_sta)
    hops = sorted({hop for _, _, hop in plan})
    barrier = pltpu.get_barrier_semaphore()
    for hop in hops:
        pl.semaphore_signal(
            barrier, inc=1, device_id=(jnp.bitwise_xor(sta, hop), stk), device_id_type=MESH
        )
    for other in range(1, n_stk):
        pl.semaphore_signal(
            barrier, inc=1, device_id=(sta, jnp.bitwise_xor(stk, other)), device_id_type=MESH
        )

    stations, _, bins = x_ref.shape[1:]
    rows = bins // LANES
    for s in range(stations):
        for a in range(rows):
            stage[s, :, a, :] = x_ref[0, s, :, a * LANES : (a + 1) * LANES]
    for s in range(stations):
        re = stage[s, 0]
        im = stage[s, 1]
        power = re * re + im * im
        level = jnp.sum(power, keepdims=True) * (1.0 / bins)
        denom = jnp.sqrt(power + 0.05 * (level + 1e-06))
        slots[0, s, 0] = (re / denom).astype(jnp.bfloat16)
        slots[0, s, 1] = (im / denom).astype(jnp.bfloat16)

    pl.semaphore_wait(barrier, len(hops) + n_stk - 1)

    def link(d, parent, hop):
        return pltpu.make_async_remote_copy(
            src_ref=slots.at[parent],
            dst_ref=slots.at[d],
            send_sem=send_sem.at[d],
            recv_sem=recv_sem.at[d],
            device_id=(jnp.bitwise_xor(sta, hop), stk),
            device_id_type=MESH,
        )

    copies = {d: link(d, parent, hop) for d, parent, hop in plan}
    children = {}
    for d, parent, _ in plan:
        children.setdefault(parent, []).append(d)
    for d in children[0]:
        copies[d].start()

    own_ref[stk] = slots[0]
    own_copies = []
    for other in range(1, n_stk):
        peer = (sta, jnp.bitwise_xor(stk, other))
        copy = pltpu.make_async_remote_copy(
            src_ref=slots.at[0],
            dst_ref=own_ref.at[stk],
            send_sem=own_send.at[other],
            recv_sem=own_recv.at[other],
            device_id=peer,
            device_id_type=MESH,
        )
        copy.start()
        own_copies.append(copy)

    for d, _, _ in plan:
        copies[d].wait_recv()
        for child in children.get(d, []):
            copies[child].start()

    far_copies = []
    for r in range(far_ref.shape[1]):
        far_ref[stk, r] = slots[mask_ref[r]]
    for other in range(1, n_stk):
        copy = pltpu.make_async_remote_copy(
            src_ref=far_ref.at[stk],
            dst_ref=far_ref.at[stk],
            send_sem=far_send.at[other],
            recv_sem=far_recv.at[other],
            device_id=(sta, jnp.bitwise_xor(stk, other)),
            device_id_type=MESH,
        )
        copy.start()
        far_copies.append(copy)
    for d, _, _ in plan:
        copies[d].wait_send()
    for copy in own_copies + far_copies:
        copy.wait()


def split(value):
    high = value.astype(jnp.bfloat16)
    low = (value - high.astype(jnp.float32)).astype(jnp.bfloat16)
    return high, low


def transform_kernel(
    n_stk, own_ref, far_ref, first_ref, twist_ref, last_ref, weight_ref, out_ref, lagged
):
    stk = lax.axis_index("stk")
    pairs, rounds, lags = out_ref.shape
    stations = far_ref.shape[2]
    weight = weight_ref[...]
    twist_re = twist_ref[0]
    twist_im = twist_ref[1]
    lane = lax.broadcasted_iota(jnp.int32, (GROUP_ROWS, LANES), 1)
    for p in range(pairs):
        pair = stk * pairs + p
        i = pair // stations
        j = lax.rem(pair, stations)
        own = [
            [own_ref[w, i, c].astype(jnp.float32) * weight for c in range(2)]
            for w in range(n_stk)
        ]
        blocks = []
        for r in range(rounds):
            re = im = None
            for w in range(n_stk):
                ar, ai = own[w]
                br = far_ref[w, r, j, 0].astype(jnp.float32)
                bi = far_ref[w, r, j, 1].astype(jnp.float32)
                re_w = ar * br + ai * bi
                im_w = ai * br - ar * bi
                re = re_w if re is None else re + re_w
                im = im_w if im is None else im + im_w
            re_high, re_low = split(re)
            im_high, im_low = split(im)
            blocks.append(
                jnp.concatenate([re_high, im_high, re_low, im_low, re_high, im_high], axis=0)
            )
        inner = jnp.dot(
            first_ref[...], jnp.concatenate(blocks, axis=1), preferred_element_type=jnp.float32
        )
        highs, lows = [], []
        for r in range(rounds):
            in_re = inner[:FINE, r * LANES : (r + 1) * LANES]
            in_im = inner[FINE:, r * LANES : (r + 1) * LANES]
            turned = jnp.concatenate(
                [in_re * twist_re - in_im * twist_im, in_re * twist_im + in_im * twist_re], axis=1
            )
            high, low = split(turned)
            highs.append(high)
            lows.append(low)
        contract = (((1,), (1,)), ((), ()))
        both = lax.dot_general(
            last_ref[...], jnp.concatenate(highs, axis=0), contract,
            preferred_element_type=jnp.float32,
        )
        rest = lax.dot_general(
            last_ref[: 2 * GROUP_ROWS], jnp.concatenate(lows, axis=0), contract,
            preferred_element_type=jnp.float32,
        )
        series = both[: 2 * GROUP_ROWS] + both[2 * GROUP_ROWS :] + rest
        for half in range(rounds // 2):
            even = series[:GROUP_ROWS, half * LANES : (half + 1) * LANES]
            odd = series[GROUP_ROWS:, half * LANES : (half + 1) * LANES]
            first = jnp.where(lane < FINE, even, pltpu.roll(odd, FINE, 1))
            second = jnp.where(lane < FINE, pltpu.roll(even, FINE, 1), odd)
            base = (p * rounds + 2 * half) * GROUP_ROWS
            lagged[base : base + GROUP_ROWS] = first
            lagged[base + GROUP_ROWS : base + 2 * GROUP_ROWS] = second
        for g in range(GROUPS):
            width = min(LANES, lags - g * LANES)
            rows = lagged[pl.ds(p * rounds * GROUP_ROWS + g, rounds, stride=GROUP_ROWS), :]
            out_ref[p, :, g * LANES : g * LANES + width] = rows[:, :width]


def turn(product):
    return np.remainder(product, NFFT) * (2.0 * math.pi / NFFT)


def tables(bins, windows):
    a = np.arange(bins // LANES)
    f = np.arange(FINE)
    c = np.arange(LANES)
    scale = 2.0 / math.sqrt(windows * bins)
    angle = turn(LANES * a[None, :] * (f[:, None] - MAXLAG))
    cos, sin = np.cos(angle), np.sin(angle)
    first = np.block([[cos, -sin], [sin, cos]]).astype(np.float32)
    angle = turn(c[None, :] * (f[:, None] - MAXLAG))
    twist = (np.stack([np.cos(angle), np.sin(angle)]) * scale).astype(np.float32)
    group = np.zeros((2, GROUP_ROWS), np.int64)
    group[0, :GROUPS] = 2 * np.arange(GROUPS)
    group[1, :GROUPS] = 2 * np.arange(GROUPS) + 1
    angle = turn(FINE * group.reshape(-1)[:, None] * c[None, :])
    last = np.concatenate([np.cos(angle), -np.sin(angle)], axis=1).astype(np.float32)
    weight = np.ones((bins // LANES, LANES), np.float32)
    weight[0, 0] = 0.5

    def halves(table):
        high = table.astype(ml_dtypes.bfloat16)
        return high, (table - high.astype(np.float32)).astype(ml_dtypes.bfloat16)

    first_high, first_low = halves(first)
    last_high, last_low = halves(last)
    return (
        np.concatenate([first_high, first_high, first_low], axis=1),
        twist,
        np.concatenate([last_high, last_low], axis=0),
        weight,
    )


def body(n_sta, n_stk, spectra, partner_masks):
    _, stations, parts, bins = spectra.shape
    rounds = partner_masks.shape[0]
    rows = bins // LANES
    block = (stations, parts, rows, LANES)
    own, far = pl.pallas_call(
        functools.partial(gather_kernel, n_sta, n_stk),
        out_shape=[
            jax.ShapeDtypeStruct((n_stk,) + block, jnp.bfloat16),
            jax.ShapeDtypeStruct((n_stk, rounds) + block, jnp.bfloat16),
        ],
        in_specs=[VMEM, pl.BlockSpec(memory_space=pltpu.SMEM)],
        out_specs=[VMEM, VMEM],
        scratch_shapes=[
            pltpu.VMEM(block, jnp.float32),
            pltpu.VMEM((n_sta,) + block, jnp.bfloat16),
            pltpu.SemaphoreType.DMA((n_sta,)),
            pltpu.SemaphoreType.DMA((n_sta,)),
            pltpu.SemaphoreType.DMA((n_stk,)),
            pltpu.SemaphoreType.DMA((n_stk,)),
            pltpu.SemaphoreType.DMA((n_stk,)),
            pltpu.SemaphoreType.DMA((n_stk,)),
        ],
        compiler_params=pltpu.CompilerParams(
            collective_id=0, has_side_effects=True, vmem_limit_bytes=32 * 2**20
        ),
        name="whiten_gather",
    )(spectra, partner_masks)
    pairs = stations * stations // n_stk
    return pl.pallas_call(
        functools.partial(transform_kernel, n_stk),
        out_shape=jax.ShapeDtypeStruct((pairs, rounds, 2 * MAXLAG), jnp.float32),
        in_specs=[VMEM] * 6,
        out_specs=VMEM,
        scratch_shapes=[pltpu.VMEM((pairs * rounds * GROUP_ROWS, LANES), jnp.float32)],
        compiler_params=pltpu.CompilerParams(vmem_limit_bytes=32 * 2**20),
        name="cross_transform",
    )(own, far, *tables(bins, n_stk))


def solution(mesh):
    return jax.shard_map(
        functools.partial(body, mesh.shape["sta"], mesh.shape["stk"]),
        mesh=mesh,
        in_specs=(P("stk", "sta", None, None), P()),
        out_specs=P(("sta", "stk"), None, None),
        check_vma=False,
    )
```

```python
import functools
import math

import jax
import jax.numpy as jnp
import ml_dtypes
import numpy as np
from jax import lax
from jax.experimental import pallas as pl
from jax.experimental.pallas import tpu as pltpu
from jax.sharding import PartitionSpec as P

NFFT = 8192
MAXLAG = 1200
LANES = 128
FINE = NFFT // LANES
GROUPS = -(-2 * MAXLAG // LANES)
GROUP_ROWS = -(-GROUPS // 8) * 8
MESH = pl.DeviceIdType.MESH
VMEM = pl.BlockSpec(memory_space=pltpu.VMEM)


def routes(count):
    plan = []
    for high in range(0, count, 4):
        if high:
            plan.append((high, 0, high))
    for high in range(0, count, 4):
        for low in (3, 1, 2):
            plan.append((high | low, high, low))
    return plan


def gather_kernel(
    n_sta, n_stk, x_ref, mask_ref, first_ref, twist_ref, last_ref,
    own_ref, far_ref, first_out, twist_out, last_out,
    x_here, masks, first_here, last_here, stage, slots, load_sem,
    send_sem, recv_sem, own_send, own_recv, far_send, far_recv,
):
    sta = lax.axis_index("sta")
    stk = lax.axis_index("stk")
    plan = routes(n_sta)
    hops = sorted({hop for _, _, hop in plan})
    sources = (x_ref, mask_ref, first_ref, twist_ref, last_ref)
    targets = (x_here, masks, first_here, twist_out, last_here)
    loads = [
        pltpu.make_async_copy(source, target, load_sem.at[index])
        for index, (source, target) in enumerate(zip(sources, targets))
    ]
    for load in loads:
        load.start()
    barrier = pltpu.get_barrier_semaphore()
    for hop in hops:
        pl.semaphore_signal(
            barrier, inc=1, device_id=(jnp.bitwise_xor(sta, hop), stk), device_id_type=MESH
        )
    for other in range(1, n_stk):
        pl.semaphore_signal(
            barrier, inc=1, device_id=(sta, jnp.bitwise_xor(stk, other)), device_id_type=MESH
        )

    loads[0].wait()
    _, stations, _, bins = x_here.shape
    rows = bins // LANES
    for s in range(stations):
        for a in range(rows):
            stage[s, :, a, :] = x_here[0, s, :, a * LANES : (a + 1) * LANES]
    for s in range(stations):
        re = stage[s, 0]
        im = stage[s, 1]
        power = re * re + im * im
        level = jnp.sum(power, keepdims=True) * (1.0 / bins)
        denom = jnp.sqrt(power + 0.05 * (level + 1e-06))
        slots[0, s, 0] = (re / denom).astype(jnp.bfloat16)
        slots[0, s, 1] = (im / denom).astype(jnp.bfloat16)

    pl.semaphore_wait(barrier, len(hops) + n_stk - 1)

    def link(d, parent, hop):
        return pltpu.make_async_remote_copy(
            src_ref=slots.at[parent],
            dst_ref=slots.at[d],
            send_sem=send_sem.at[d],
            recv_sem=recv_sem.at[d],
            device_id=(jnp.bitwise_xor(sta, hop), stk),
            device_id_type=MESH,
        )

    copies = {d: link(d, parent, hop) for d, parent, hop in plan}
    children = {}
    for d, parent, _ in plan:
        children.setdefault(parent, []).append(d)
    for d in children[0]:
        copies[d].start()

    own_ref[stk] = slots[0]
    own_copies = []
    for other in range(1, n_stk):
        peer = (sta, jnp.bitwise_xor(stk, other))
        copy = pltpu.make_async_remote_copy(
            src_ref=slots.at[0],
            dst_ref=own_ref.at[stk],
            send_sem=own_send.at[other],
            recv_sem=own_recv.at[other],
            device_id=peer,
            device_id_type=MESH,
        )
        copy.start()
        own_copies.append(copy)

    for load in loads[1:]:
        load.wait()
    first_out[...] = first_here[...].astype(jnp.bfloat16)
    last_out[...] = last_here[...].astype(jnp.bfloat16)

    for d, _, _ in plan:
        copies[d].wait_recv()
        for child in children.get(d, []):
            copies[child].start()

    far_copies = []
    for r in range(far_ref.shape[1]):
        far_ref[stk, r] = slots[masks[r]]
    for other in range(1, n_stk):
        copy = pltpu.make_async_remote_copy(
            src_ref=far_ref.at[stk],
            dst_ref=far_ref.at[stk],
            send_sem=far_send.at[other],
            recv_sem=far_recv.at[other],
            device_id=(sta, jnp.bitwise_xor(stk, other)),
            device_id_type=MESH,
        )
        copy.start()
        far_copies.append(copy)
    for d, _, _ in plan:
        copies[d].wait_send()
    for copy in own_copies + far_copies:
        copy.wait()


def split(value):
    high = value.astype(jnp.bfloat16)
    low = (value - high.astype(jnp.float32)).astype(jnp.bfloat16)
    return high, low


def transform_kernel(
    n_stk, own_ref, far_ref, first_ref, twist_ref, last_ref, out_ref, lagged
):
    stk = lax.axis_index("stk")
    pairs, rounds, lags = out_ref.shape
    stations = far_ref.shape[2]
    grid = far_ref.shape[4:]
    bin_index = LANES * lax.broadcasted_iota(jnp.int32, grid, 0) + lax.broadcasted_iota(
        jnp.int32, grid, 1
    )
    weight = jnp.where(bin_index == 0, 0.5, 1.0).astype(jnp.float32)
    twist_re = twist_ref[0]
    twist_im = twist_ref[1]
    lane = lax.broadcasted_iota(jnp.int32, (GROUP_ROWS, LANES), 1)
    for p in range(pairs):
        pair = stk * pairs + p
        i = pair // stations
        j = lax.rem(pair, stations)
        own = [
            [own_ref[w, i, c].astype(jnp.float32) * weight for c in range(2)]
            for w in range(n_stk)
        ]
        blocks = []
        for r in range(rounds):
            re = im = None
            for w in range(n_stk):
                ar, ai = own[w]
                br = far_ref[w, r, j, 0].astype(jnp.float32)
                bi = far_ref[w, r, j, 1].astype(jnp.float32)
                re_w = ar * br + ai * bi
                im_w = ai * br - ar * bi
                re = re_w if re is None else re + re_w
                im = im_w if im is None else im + im_w
            re_high, re_low = split(re)
            im_high, im_low = split(im)
            blocks.append(
                jnp.concatenate([re_high, im_high, re_low, im_low, re_high, im_high], axis=0)
            )
        inner = jnp.dot(
            first_ref[...], jnp.concatenate(blocks, axis=1), preferred_element_type=jnp.float32
        )
        highs, lows = [], []
        for r in range(rounds):
            in_re = inner[:FINE, r * LANES : (r + 1) * LANES]
            in_im = inner[FINE:, r * LANES : (r + 1) * LANES]
            turned = jnp.concatenate(
                [in_re * twist_re - in_im * twist_im, in_re * twist_im + in_im * twist_re], axis=1
            )
            high, low = split(turned)
            highs.append(high)
            lows.append(low)
        contract = (((1,), (1,)), ((), ()))
        both = lax.dot_general(
            last_ref[...], jnp.concatenate(highs, axis=0), contract,
            preferred_element_type=jnp.float32,
        )
        rest = lax.dot_general(
            last_ref[: 2 * GROUP_ROWS], jnp.concatenate(lows, axis=0), contract,
            preferred_element_type=jnp.float32,
        )
        series = both[: 2 * GROUP_ROWS] + both[2 * GROUP_ROWS :] + rest
        for half in range(rounds // 2):
            even = series[:GROUP_ROWS, half * LANES : (half + 1) * LANES]
            odd = series[GROUP_ROWS:, half * LANES : (half + 1) * LANES]
            first = jnp.where(lane < FINE, even, pltpu.roll(odd, FINE, 1))
            second = jnp.where(lane < FINE, pltpu.roll(even, FINE, 1), odd)
            base = (p * rounds + 2 * half) * GROUP_ROWS
            lagged[base : base + GROUP_ROWS] = first
            lagged[base + GROUP_ROWS : base + 2 * GROUP_ROWS] = second
        for g in range(GROUPS):
            width = min(LANES, lags - g * LANES)
            rows = lagged[pl.ds(p * rounds * GROUP_ROWS + g, rounds, stride=GROUP_ROWS), :]
            out_ref[p, :, g * LANES : g * LANES + width] = rows[:, :width]


def turn(product):
    return np.remainder(product, NFFT) * (2.0 * math.pi / NFFT)


def tables(bins, windows):
    a = np.arange(bins // LANES)
    f = np.arange(FINE)
    c = np.arange(LANES)
    scale = 2.0 / math.sqrt(windows * bins)
    angle = turn(LANES * a[None, :] * (f[:, None] - MAXLAG))
    cos, sin = np.cos(angle), np.sin(angle)
    first = np.block([[cos, -sin], [sin, cos]]).astype(np.float32)
    angle = turn(c[None, :] * (f[:, None] - MAXLAG))
    twist = (np.stack([np.cos(angle), np.sin(angle)]) * scale).astype(np.float32)
    group = np.zeros((2, GROUP_ROWS), np.int64)
    group[0, :GROUPS] = 2 * np.arange(GROUPS)
    group[1, :GROUPS] = 2 * np.arange(GROUPS) + 1
    angle = turn(FINE * group.reshape(-1)[:, None] * c[None, :])
    last = np.concatenate([np.cos(angle), -np.sin(angle)], axis=1).astype(np.float32)

    def halves(table):
        high = table.astype(ml_dtypes.bfloat16).astype(np.float32)
        return high, (table - high).astype(ml_dtypes.bfloat16).astype(np.float32)

    first_high, first_low = halves(first)
    last_high, last_low = halves(last)
    return (
        np.concatenate([first_high, first_high, first_low], axis=1),
        twist,
        np.concatenate([last_high, last_low], axis=0),
    )


def body(n_sta, n_stk, spectra, partner_masks):
    _, stations, parts, bins = spectra.shape
    rounds = partner_masks.shape[0]
    rows = bins // LANES
    block = (stations, parts, rows, LANES)
    fixed = tables(bins, n_stk)
    first_shape, twist_shape, last_shape = [table.shape for table in fixed]
    operands = [
        pltpu.with_memory_space_constraint(jnp.asarray(operand), pltpu.HBM)
        for operand in (spectra, partner_masks, *fixed)
    ]
    own, far, first, twist, last = pl.pallas_call(
        functools.partial(gather_kernel, n_sta, n_stk),
        out_shape=[
            jax.ShapeDtypeStruct((n_stk,) + block, jnp.bfloat16),
            jax.ShapeDtypeStruct((n_stk, rounds) + block, jnp.bfloat16),
            jax.ShapeDtypeStruct(first_shape, jnp.bfloat16),
            jax.ShapeDtypeStruct(twist_shape, jnp.float32),
            jax.ShapeDtypeStruct(last_shape, jnp.bfloat16),
        ],
        in_specs=[pl.BlockSpec(memory_space=pltpu.HBM)] * 5,
        out_specs=[VMEM] * 5,
        scratch_shapes=[
            pltpu.VMEM(spectra.shape, jnp.float32),
            pltpu.SMEM((rounds,), jnp.int32),
            pltpu.VMEM(first_shape, jnp.float32),
            pltpu.VMEM(last_shape, jnp.float32),
            pltpu.VMEM(block, jnp.float32),
            pltpu.VMEM((n_sta,) + block, jnp.bfloat16),
            pltpu.SemaphoreType.DMA((5,)),
            pltpu.SemaphoreType.DMA((n_sta,)),
            pltpu.SemaphoreType.DMA((n_sta,)),
            pltpu.SemaphoreType.DMA((n_stk,)),
            pltpu.SemaphoreType.DMA((n_stk,)),
            pltpu.SemaphoreType.DMA((n_stk,)),
            pltpu.SemaphoreType.DMA((n_stk,)),
        ],
        compiler_params=pltpu.CompilerParams(
            collective_id=0, has_side_effects=True, vmem_limit_bytes=32 * 2**20
        ),
        name="whiten_gather",
    )(*operands)
    pairs = stations * stations // n_stk
    return pl.pallas_call(
        functools.partial(transform_kernel, n_stk),
        out_shape=jax.ShapeDtypeStruct((pairs, rounds, 2 * MAXLAG), jnp.float32),
        in_specs=[VMEM] * 5,
        out_specs=VMEM,
        scratch_shapes=[pltpu.VMEM((pairs * rounds * GROUP_ROWS, LANES), jnp.float32)],
        compiler_params=pltpu.CompilerParams(vmem_limit_bytes=32 * 2**20),
        name="cross_transform",
    )(own, far, first, twist, last)


def solution(mesh):
    return jax.shard_map(
        functools.partial(body, mesh.shape["sta"], mesh.shape["stk"]),
        mesh=mesh,
        in_specs=(P("stk", "sta", None, None), P()),
        out_specs=P(("sta", "stk"), None, None),
        check_vma=False,
    )
```

```python
import functools
import math

import jax
import jax.numpy as jnp
import ml_dtypes
import numpy as np
from jax import lax
from jax.experimental import pallas as pl
from jax.experimental.pallas import tpu as pltpu
from jax.sharding import PartitionSpec as P

NFFT = 8192
MAXLAG = 1200
LANES = 128
FINE = NFFT // LANES
GROUPS = -(-2 * MAXLAG // LANES)
GROUP_ROWS = -(-GROUPS // 8) * 8
MESH = pl.DeviceIdType.MESH
VMEM = pl.BlockSpec(memory_space=pltpu.VMEM)


def routes(count):
    near = {1: 0, 2: 0, 4: 0, 6: 4, 3: 2, 5: 1, 7: 6}
    plan = [(d, near[d], d ^ near[d]) for d in (1, 2, 4) if d < count]
    plan += [(top, 0, top) for top in range(8, count, 8)]
    plan += [(d, near[d], d ^ near[d]) for d in (6, 3, 5, 7) if d < count]
    plan += [(top | low, top, low) for top in range(8, count, 8) for low in (4, 1, 2, 3, 5, 6, 7)]
    return plan


def gather_kernel(
    n_sta, n_stk, x_ref, mask_ref, first_ref, twist_ref, last_ref,
    own_ref, far_ref, first_out, twist_out, last_out,
    x_here, masks, first_here, last_here, stage, slots, load_sem,
    send_sem, recv_sem, twin_send, twin_recv,
):
    sta = lax.axis_index("sta")
    stk = lax.axis_index("stk")
    plan = routes(n_sta)
    hops = sorted({hop for _, _, hop in plan})
    sources = (x_ref, mask_ref, first_ref, twist_ref, last_ref)
    targets = (x_here, masks, first_here, twist_out, last_here)
    loads = [
        pltpu.make_async_copy(source, target, load_sem.at[index])
        for index, (source, target) in enumerate(zip(sources, targets))
    ]
    for load in loads:
        load.start()
    barrier = pltpu.get_barrier_semaphore()
    for hop in hops:
        pl.semaphore_signal(
            barrier, inc=1, device_id=(jnp.bitwise_xor(sta, hop), stk), device_id_type=MESH
        )
    for other in range(1, n_stk):
        pl.semaphore_signal(
            barrier, inc=1, device_id=(sta, jnp.bitwise_xor(stk, other)), device_id_type=MESH
        )

    loads[0].wait()
    _, stations, _, bins = x_here.shape
    rows = bins // LANES
    for s in range(stations):
        for a in range(rows):
            stage[s, :, a, :] = x_here[0, s, :, a * LANES : (a + 1) * LANES]
    for s in range(stations):
        re = stage[s, 0]
        im = stage[s, 1]
        power = re * re + im * im
        level = jnp.sum(power, keepdims=True) * (1.0 / bins)
        denom = jnp.sqrt(power + 0.05 * (level + 1e-06))
        slots[stk, 0, s, 0] = (re / denom).astype(jnp.bfloat16)
        slots[stk, 0, s, 1] = (im / denom).astype(jnp.bfloat16)

    pl.semaphore_wait(barrier, len(hops) + n_stk - 1)

    def link(d, parent, hop):
        return pltpu.make_async_remote_copy(
            src_ref=slots.at[stk, parent],
            dst_ref=slots.at[stk, d],
            send_sem=send_sem.at[d],
            recv_sem=recv_sem.at[d],
            device_id=(jnp.bitwise_xor(sta, hop), stk),
            device_id_type=MESH,
        )

    def twin(d, other):
        return pltpu.make_async_remote_copy(
            src_ref=slots.at[stk, d],
            dst_ref=slots.at[stk, d],
            send_sem=twin_send.at[d, other],
            recv_sem=twin_recv.at[d, other],
            device_id=(sta, jnp.bitwise_xor(stk, other)),
            device_id_type=MESH,
        )

    copies = {d: link(d, parent, hop) for d, parent, hop in plan}
    twins = [twin(d, other) for d in range(n_sta) for other in range(1, n_stk)]
    children = {}
    for d, parent, _ in plan:
        children.setdefault(parent, []).append(d)

    def pass_on(d):
        for child in sorted(children.get(d, []), reverse=d == 0):
            copies[child].start()
        for copy in twins[d * (n_stk - 1) : (d + 1) * (n_stk - 1)]:
            copy.start()

    pass_on(0)
    for load in loads[1:]:
        load.wait()
    first_out[...] = first_here[...].astype(jnp.bfloat16)
    last_out[...] = last_here[...].astype(jnp.bfloat16)

    for d, _, _ in plan:
        copies[d].wait_recv()
        pass_on(d)
    for copy in twins:
        copy.wait_recv()
    for w in range(n_stk):
        own_ref[w] = slots[w, 0]
        for r in range(far_ref.shape[1]):
            far_ref[w, r] = slots[w, masks[r]]
    for d, _, _ in plan:
        copies[d].wait_send()
    for copy in twins:
        copy.wait_send()


def split(value):
    high = value.astype(jnp.bfloat16)
    low = (value - high.astype(jnp.float32)).astype(jnp.bfloat16)
    return high, low


def transform_kernel(
    n_stk, own_ref, far_ref, first_ref, twist_ref, last_ref, out_ref, lagged
):
    stk = lax.axis_index("stk")
    pairs, rounds, lags = out_ref.shape
    stations = far_ref.shape[2]
    grid = far_ref.shape[4:]
    bin_index = LANES * lax.broadcasted_iota(jnp.int32, grid, 0) + lax.broadcasted_iota(
        jnp.int32, grid, 1
    )
    weight = jnp.where(bin_index == 0, 0.5, 1.0).astype(jnp.float32)
    twist_re = twist_ref[0]
    twist_im = twist_ref[1]
    lane = lax.broadcasted_iota(jnp.int32, (GROUP_ROWS, LANES), 1)
    for p in range(pairs):
        pair = stk * pairs + p
        i = pair // stations
        j = lax.rem(pair, stations)
        own = [
            [own_ref[w, i, c].astype(jnp.float32) * weight for c in range(2)]
            for w in range(n_stk)
        ]
        blocks = []
        for r in range(rounds):
            re = im = None
            for w in range(n_stk):
                ar, ai = own[w]
                br = far_ref[w, r, j, 0].astype(jnp.float32)
                bi = far_ref[w, r, j, 1].astype(jnp.float32)
                re_w = ar * br + ai * bi
                im_w = ai * br - ar * bi
                re = re_w if re is None else re + re_w
                im = im_w if im is None else im + im_w
            re_high, re_low = split(re)
            im_high, im_low = split(im)
            blocks.append(
                jnp.concatenate([re_high, im_high, re_low, im_low, re_high, im_high], axis=0)
            )
        inner = jnp.dot(
            first_ref[...], jnp.concatenate(blocks, axis=1), preferred_element_type=jnp.float32
        )
        highs, lows = [], []
        for r in range(rounds):
            in_re = inner[:FINE, r * LANES : (r + 1) * LANES]
            in_im = inner[FINE:, r * LANES : (r + 1) * LANES]
            turned = jnp.concatenate(
                [in_re * twist_re - in_im * twist_im, in_re * twist_im + in_im * twist_re], axis=1
            )
            high, low = split(turned)
            highs.append(high)
            lows.append(low)
        contract = (((1,), (1,)), ((), ()))
        both = lax.dot_general(
            last_ref[...], jnp.concatenate(highs, axis=0), contract,
            preferred_element_type=jnp.float32,
        )
        rest = lax.dot_general(
            last_ref[: 2 * GROUP_ROWS], jnp.concatenate(lows, axis=0), contract,
            preferred_element_type=jnp.float32,
        )
        series = both[: 2 * GROUP_ROWS] + both[2 * GROUP_ROWS :] + rest
        for half in range(rounds // 2):
            even = series[:GROUP_ROWS, half * LANES : (half + 1) * LANES]
            odd = series[GROUP_ROWS:, half * LANES : (half + 1) * LANES]
            first = jnp.where(lane < FINE, even, pltpu.roll(odd, FINE, 1))
            second = jnp.where(lane < FINE, pltpu.roll(even, FINE, 1), odd)
            base = (p * rounds + 2 * half) * GROUP_ROWS
            lagged[base : base + GROUP_ROWS] = first
            lagged[base + GROUP_ROWS : base + 2 * GROUP_ROWS] = second
        for g in range(GROUPS):
            width = min(LANES, lags - g * LANES)
            rows = lagged[pl.ds(p * rounds * GROUP_ROWS + g, rounds, stride=GROUP_ROWS), :]
            out_ref[p, :, g * LANES : g * LANES + width] = rows[:, :width]


def turn(product):
    return np.remainder(product, NFFT) * (2.0 * math.pi / NFFT)


def tables(bins, windows):
    a = np.arange(bins // LANES)
    f = np.arange(FINE)
    c = np.arange(LANES)
    scale = 2.0 / math.sqrt(windows * bins)
    angle = turn(LANES * a[None, :] * (f[:, None] - MAXLAG))
    cos, sin = np.cos(angle), np.sin(angle)
    first = np.block([[cos, -sin], [sin, cos]]).astype(np.float32)
    angle = turn(c[None, :] * (f[:, None] - MAXLAG))
    twist = (np.stack([np.cos(angle), np.sin(angle)]) * scale).astype(np.float32)
    group = np.zeros((2, GROUP_ROWS), np.int64)
    group[0, :GROUPS] = 2 * np.arange(GROUPS)
    group[1, :GROUPS] = 2 * np.arange(GROUPS) + 1
    angle = turn(FINE * group.reshape(-1)[:, None] * c[None, :])
    last = np.concatenate([np.cos(angle), -np.sin(angle)], axis=1).astype(np.float32)

    def halves(table):
        high = table.astype(ml_dtypes.bfloat16).astype(np.float32)
        return high, (table - high).astype(ml_dtypes.bfloat16).astype(np.float32)

    first_high, first_low = halves(first)
    last_high, last_low = halves(last)
    return (
        np.concatenate([first_high, first_high, first_low], axis=1),
        twist,
        np.concatenate([last_high, last_low], axis=0),
    )


def body(n_sta, n_stk, spectra, partner_masks):
    _, stations, parts, bins = spectra.shape
    rounds = partner_masks.shape[0]
    rows = bins // LANES
    block = (stations, parts, rows, LANES)
    fixed = tables(bins, n_stk)
    first_shape, twist_shape, last_shape = [table.shape for table in fixed]
    operands = [
        pltpu.with_memory_space_constraint(jnp.asarray(operand), pltpu.HBM)
        for operand in (spectra, partner_masks, *fixed)
    ]
    own, far, first, twist, last = pl.pallas_call(
        functools.partial(gather_kernel, n_sta, n_stk),
        out_shape=[
            jax.ShapeDtypeStruct((n_stk,) + block, jnp.bfloat16),
            jax.ShapeDtypeStruct((n_stk, rounds) + block, jnp.bfloat16),
            jax.ShapeDtypeStruct(first_shape, jnp.bfloat16),
            jax.ShapeDtypeStruct(twist_shape, jnp.float32),
            jax.ShapeDtypeStruct(last_shape, jnp.bfloat16),
        ],
        in_specs=[pl.BlockSpec(memory_space=pltpu.HBM)] * 5,
        out_specs=[VMEM] * 5,
        scratch_shapes=[
            pltpu.VMEM(spectra.shape, jnp.float32),
            pltpu.SMEM((rounds,), jnp.int32),
            pltpu.VMEM(first_shape, jnp.float32),
            pltpu.VMEM(last_shape, jnp.float32),
            pltpu.VMEM(block, jnp.float32),
            pltpu.VMEM((n_stk, n_sta) + block, jnp.bfloat16),
            pltpu.SemaphoreType.DMA((5,)),
            pltpu.SemaphoreType.DMA((n_sta,)),
            pltpu.SemaphoreType.DMA((n_sta,)),
            pltpu.SemaphoreType.DMA((n_sta, n_stk)),
            pltpu.SemaphoreType.DMA((n_sta, n_stk)),
        ],
        compiler_params=pltpu.CompilerParams(
            collective_id=0, has_side_effects=True, vmem_limit_bytes=32 * 2**20
        ),
        name="whiten_gather",
    )(*operands)
    pairs = stations * stations // n_stk
    return pl.pallas_call(
        functools.partial(transform_kernel, n_stk),
        out_shape=jax.ShapeDtypeStruct((pairs, rounds, 2 * MAXLAG), jnp.float32),
        in_specs=[VMEM] * 5,
        out_specs=VMEM,
        scratch_shapes=[pltpu.VMEM((pairs * rounds * GROUP_ROWS, LANES), jnp.float32)],
        compiler_params=pltpu.CompilerParams(vmem_limit_bytes=32 * 2**20),
        name="cross_transform",
    )(own, far, first, twist, last)


def solution(mesh):
    return jax.shard_map(
        functools.partial(body, mesh.shape["sta"], mesh.shape["stk"]),
        mesh=mesh,
        in_specs=(P("stk", "sta", None, None), P()),
        out_specs=P(("sta", "stk"), None, None),
        check_vma=False,
    )
```

```python
import functools
import math

import jax
import jax.numpy as jnp
import ml_dtypes
import numpy as np
from jax import lax
from jax.experimental import pallas as pl
from jax.experimental.pallas import tpu as pltpu
from jax.sharding import PartitionSpec as P

NFFT = 8192
MAXLAG = 1200
LANES = 128
FINE = NFFT // LANES
GROUPS = -(-2 * MAXLAG // LANES)
GROUP_ROWS = -(-GROUPS // 8) * 8
HALVES = 2
MESH = pl.DeviceIdType.MESH
VMEM = pl.BlockSpec(memory_space=pltpu.VMEM)


def routes(count):
    plan = []
    for high in range(0, count, 4):
        if high:
            plan.append((high, 0, high))
    for high in range(0, count, 4):
        for low in (3, 1, 2):
            plan.append((high | low, high, low))
    return plan


def gather_kernel(
    n_sta, n_stk, x_ref, mask_ref, first_ref, twist_ref, last_ref,
    own_ref, far_ref, first_out, twist_out, last_out,
    x_here, masks, first_here, last_here, stage, slots, load_sem,
    send_sem, recv_sem, own_send, own_recv, far_send, far_recv,
):
    sta = lax.axis_index("sta")
    stk = lax.axis_index("stk")
    plan = routes(n_sta)
    hops = sorted({hop for _, _, hop in plan})
    sources = (mask_ref, first_ref, twist_ref, last_ref)
    targets = (masks, first_here, twist_out, last_here)
    stations = x_here.shape[1]
    parts = [pl.ds(half * (stations // HALVES), stations // HALVES) for half in range(HALVES)]
    loads = [
        pltpu.make_async_copy(x_ref.at[:, part], x_here.at[:, part], load_sem.at[half])
        for half, part in enumerate(parts)
    ]
    loads += [
        pltpu.make_async_copy(source, target, load_sem.at[HALVES + index])
        for index, (source, target) in enumerate(zip(sources, targets))
    ]
    for load in loads:
        load.start()
    barrier = pltpu.get_barrier_semaphore()
    for hop in hops:
        pl.semaphore_signal(
            barrier, inc=1, device_id=(jnp.bitwise_xor(sta, hop), stk), device_id_type=MESH
        )
    for other in range(1, n_stk):
        pl.semaphore_signal(
            barrier, inc=1, device_id=(sta, jnp.bitwise_xor(stk, other)), device_id_type=MESH
        )

    def link(d, parent, hop, half):
        return pltpu.make_async_remote_copy(
            src_ref=slots.at[parent, parts[half]],
            dst_ref=slots.at[d, parts[half]],
            send_sem=send_sem.at[d, half],
            recv_sem=recv_sem.at[d, half],
            device_id=(jnp.bitwise_xor(sta, hop), stk),
            device_id_type=MESH,
        )

    copies = {
        (d, half): link(d, parent, hop, half)
        for half in range(HALVES)
        for d, parent, hop in plan
    }
    children = {}
    for d, parent, _ in plan:
        children.setdefault(parent, []).append(d)

    bins = x_here.shape[3]
    rows = bins // LANES
    for half in range(HALVES):
        loads[half].wait()
        here = range(half * (stations // HALVES), (half + 1) * (stations // HALVES))
        for s in here:
            for a in range(rows):
                stage[s, :, a, :] = x_here[0, s, :, a * LANES : (a + 1) * LANES]
        for s in here:
            re = stage[s, 0]
            im = stage[s, 1]
            power = re * re + im * im
            level = jnp.sum(power, keepdims=True) * (1.0 / bins)
            denom = jnp.sqrt(power + 0.05 * (level + 1e-06))
            slots[0, s, 0] = (re / denom).astype(jnp.bfloat16)
            slots[0, s, 1] = (im / denom).astype(jnp.bfloat16)
        if half == 0:
            pl.semaphore_wait(barrier, len(hops) + n_stk - 1)
        for d in sorted(children[0], reverse=True):
            copies[d, half].start()

    own_ref[stk] = slots[0]
    own_copies = []
    for other in range(1, n_stk):
        peer = (sta, jnp.bitwise_xor(stk, other))
        copy = pltpu.make_async_remote_copy(
            src_ref=slots.at[0],
            dst_ref=own_ref.at[stk],
            send_sem=own_send.at[other],
            recv_sem=own_recv.at[other],
            device_id=peer,
            device_id_type=MESH,
        )
        copy.start()
        own_copies.append(copy)

    for load in loads[HALVES:]:
        load.wait()
    first_out[...] = first_here[...].astype(jnp.bfloat16)
    last_out[...] = last_here[...].astype(jnp.bfloat16)

    for d, _, _ in plan:
        for half in range(HALVES):
            copies[d, half].wait_recv()
            for child in children.get(d, []):
                copies[child, half].start()

    far_copies = []
    for r in range(far_ref.shape[1]):
        far_ref[stk, r] = slots[masks[r]]
    for other in range(1, n_stk):
        copy = pltpu.make_async_remote_copy(
            src_ref=far_ref.at[stk],
            dst_ref=far_ref.at[stk],
            send_sem=far_send.at[other],
            recv_sem=far_recv.at[other],
            device_id=(sta, jnp.bitwise_xor(stk, other)),
            device_id_type=MESH,
        )
        copy.start()
        far_copies.append(copy)
    for copy in copies.values():
        copy.wait_send()
    for copy in own_copies + far_copies:
        copy.wait()


def split(value):
    high = value.astype(jnp.bfloat16)
    low = (value - high.astype(jnp.float32)).astype(jnp.bfloat16)
    return high, low


def transform_kernel(
    n_stk, own_ref, far_ref, first_ref, twist_ref, last_ref, out_ref, result, lagged, out_sem
):
    stk = lax.axis_index("stk")
    pairs, rounds, lags = out_ref.shape
    stations = far_ref.shape[2]
    grid = far_ref.shape[4:]
    bin_index = LANES * lax.broadcasted_iota(jnp.int32, grid, 0) + lax.broadcasted_iota(
        jnp.int32, grid, 1
    )
    weight = jnp.where(bin_index == 0, 0.5, 1.0).astype(jnp.float32)
    twist_re = twist_ref[0]
    twist_im = twist_ref[1]
    lane = lax.broadcasted_iota(jnp.int32, (GROUP_ROWS, LANES), 1)
    copies = []
    for p in range(pairs):
        pair = stk * pairs + p
        i = pair // stations
        j = lax.rem(pair, stations)
        own = [
            [own_ref[w, i, c].astype(jnp.float32) * weight for c in range(2)]
            for w in range(n_stk)
        ]
        blocks = []
        for r in range(rounds):
            re = im = None
            for w in range(n_stk):
                ar, ai = own[w]
                br = far_ref[w, r, j, 0].astype(jnp.float32)
                bi = far_ref[w, r, j, 1].astype(jnp.float32)
                re_w = ar * br + ai * bi
                im_w = ai * br - ar * bi
                re = re_w if re is None else re + re_w
                im = im_w if im is None else im + im_w
            re_high, re_low = split(re)
            im_high, im_low = split(im)
            blocks.append(
                jnp.concatenate([re_high, im_high, re_low, im_low, re_high, im_high], axis=0)
            )
        inner = jnp.dot(
            first_ref[...], jnp.concatenate(blocks, axis=1), preferred_element_type=jnp.float32
        )
        highs, lows = [], []
        for r in range(rounds):
            in_re = inner[:FINE, r * LANES : (r + 1) * LANES]
            in_im = inner[FINE:, r * LANES : (r + 1) * LANES]
            turned = jnp.concatenate(
                [in_re * twist_re - in_im * twist_im, in_re * twist_im + in_im * twist_re], axis=1
            )
            high, low = split(turned)
            highs.append(high)
            lows.append(low)
        contract = (((1,), (1,)), ((), ()))
        both = lax.dot_general(
            last_ref[...], jnp.concatenate(highs, axis=0), contract,
            preferred_element_type=jnp.float32,
        )
        rest = lax.dot_general(
            last_ref[: 2 * GROUP_ROWS], jnp.concatenate(lows, axis=0), contract,
            preferred_element_type=jnp.float32,
        )
        series = both[: 2 * GROUP_ROWS] + both[2 * GROUP_ROWS :] + rest
        for half in range(rounds // 2):
            even = series[:GROUP_ROWS, half * LANES : (half + 1) * LANES]
            odd = series[GROUP_ROWS:, half * LANES : (half + 1) * LANES]
            first = jnp.where(lane < FINE, even, pltpu.roll(odd, FINE, 1))
            second = jnp.where(lane < FINE, pltpu.roll(even, FINE, 1), odd)
            base = (p * rounds + 2 * half) * GROUP_ROWS
            lagged[base : base + GROUP_ROWS] = first
            lagged[base + GROUP_ROWS : base + 2 * GROUP_ROWS] = second
        for g in range(GROUPS):
            width = min(LANES, lags - g * LANES)
            rows = lagged[pl.ds(p * rounds * GROUP_ROWS + g, rounds, stride=GROUP_ROWS), :]
            result[p, :, g * LANES : g * LANES + width] = rows[:, :width]
        copy = pltpu.make_async_copy(result.at[p], out_ref.at[p], out_sem.at[p])
        copy.start()
        copies.append(copy)
    for copy in copies:
        copy.wait()


def turn(product):
    return np.remainder(product, NFFT) * (2.0 * math.pi / NFFT)


def tables(bins, windows):
    a = np.arange(bins // LANES)
    f = np.arange(FINE)
    c = np.arange(LANES)
    scale = 2.0 / math.sqrt(windows * bins)
    angle = turn(LANES * a[None, :] * (f[:, None] - MAXLAG))
    cos, sin = np.cos(angle), np.sin(angle)
    first = np.block([[cos, -sin], [sin, cos]]).astype(np.float32)
    angle = turn(c[None, :] * (f[:, None] - MAXLAG))
    twist = (np.stack([np.cos(angle), np.sin(angle)]) * scale).astype(np.float32)
    group = np.zeros((2, GROUP_ROWS), np.int64)
    group[0, :GROUPS] = 2 * np.arange(GROUPS)
    group[1, :GROUPS] = 2 * np.arange(GROUPS) + 1
    angle = turn(FINE * group.reshape(-1)[:, None] * c[None, :])
    last = np.concatenate([np.cos(angle), -np.sin(angle)], axis=1).astype(np.float32)

    def halves(table):
        high = table.astype(ml_dtypes.bfloat16).astype(np.float32)
        return high, (table - high).astype(ml_dtypes.bfloat16).astype(np.float32)

    first_high, first_low = halves(first)
    last_high, last_low = halves(last)
    return (
        np.concatenate([first_high, first_high, first_low], axis=1),
        twist,
        np.concatenate([last_high, last_low], axis=0),
    )


def body(n_sta, n_stk, spectra, partner_masks):
    _, stations, parts, bins = spectra.shape
    rounds = partner_masks.shape[0]
    rows = bins // LANES
    block = (stations, parts, rows, LANES)
    fixed = tables(bins, n_stk)
    first_shape, twist_shape, last_shape = [table.shape for table in fixed]
    operands = [
        pltpu.with_memory_space_constraint(jnp.asarray(operand), pltpu.HBM)
        for operand in (spectra, partner_masks, *fixed)
    ]
    own, far, first, twist, last = pl.pallas_call(
        functools.partial(gather_kernel, n_sta, n_stk),
        out_shape=[
            jax.ShapeDtypeStruct((n_stk,) + block, jnp.bfloat16),
            jax.ShapeDtypeStruct((n_stk, rounds) + block, jnp.bfloat16),
            jax.ShapeDtypeStruct(first_shape, jnp.bfloat16),
            jax.ShapeDtypeStruct(twist_shape, jnp.float32),
            jax.ShapeDtypeStruct(last_shape, jnp.bfloat16),
        ],
        in_specs=[pl.BlockSpec(memory_space=pltpu.HBM)] * 5,
        out_specs=[VMEM] * 5,
        scratch_shapes=[
            pltpu.VMEM(spectra.shape, jnp.float32),
            pltpu.SMEM((rounds,), jnp.int32),
            pltpu.VMEM(first_shape, jnp.float32),
            pltpu.VMEM(last_shape, jnp.float32),
            pltpu.VMEM(block, jnp.float32),
            pltpu.VMEM((n_sta,) + block, jnp.bfloat16),
            pltpu.SemaphoreType.DMA((HALVES + 4,)),
            pltpu.SemaphoreType.DMA((n_sta, HALVES)),
            pltpu.SemaphoreType.DMA((n_sta, HALVES)),
            pltpu.SemaphoreType.DMA((n_stk,)),
            pltpu.SemaphoreType.DMA((n_stk,)),
            pltpu.SemaphoreType.DMA((n_stk,)),
            pltpu.SemaphoreType.DMA((n_stk,)),
        ],
        compiler_params=pltpu.CompilerParams(
            collective_id=0, has_side_effects=True, vmem_limit_bytes=32 * 2**20
        ),
        name="whiten_gather",
    )(*operands)
    pairs = stations * stations // n_stk
    return pl.pallas_call(
        functools.partial(transform_kernel, n_stk),
        out_shape=jax.ShapeDtypeStruct((pairs, rounds, 2 * MAXLAG), jnp.float32),
        in_specs=[VMEM] * 5,
        out_specs=pl.BlockSpec(memory_space=pltpu.HBM),
        scratch_shapes=[
            pltpu.VMEM((pairs, rounds, 2 * MAXLAG), jnp.float32),
            pltpu.VMEM((pairs * rounds * GROUP_ROWS, LANES), jnp.float32),
            pltpu.SemaphoreType.DMA((pairs,)),
        ],
        compiler_params=pltpu.CompilerParams(vmem_limit_bytes=32 * 2**20),
        name="cross_transform",
    )(own, far, first, twist, last)


def solution(mesh):
    return jax.shard_map(
        functools.partial(body, mesh.shape["sta"], mesh.shape["stk"]),
        mesh=mesh,
        in_specs=(P("stk", "sta", None, None), P()),
        out_specs=P(("sta", "stk"), None, None),
        check_vma=False,
    )
```

```python
import functools
import math

import jax
import jax.numpy as jnp
import ml_dtypes
import numpy as np
from jax import lax
from jax.experimental import pallas as pl
from jax.experimental.pallas import tpu as pltpu
from jax.sharding import PartitionSpec as P

NFFT = 8192
MAXLAG = 1200
LANES = 128
FINE = NFFT // LANES
GROUPS = -(-2 * MAXLAG // LANES)
GROUP_ROWS = -(-GROUPS // 8) * 8
MESH = pl.DeviceIdType.MESH
VMEM = pl.BlockSpec(memory_space=pltpu.VMEM)


def routes(count):
    plan = [(high, 0, high) for high in range(4, count, 4)]
    plan += [(low, 0, low) for low in (1, 2, 3)]
    plan += [(high | low, high, low) for high in range(8, count, 4) for low in (1, 2, 3)]
    plan += [(4 | low, low, 4) for low in (1, 2, 3)]
    return plan


def gather_kernel(
    n_sta, n_stk, x_ref, mask_ref, first_ref, twist_ref, last_ref,
    own_ref, far_ref, first_out, twist_out, last_out,
    x_here, masks, first_here, last_here, stage, slots, load_sem,
    send_sem, recv_sem, own_send, own_recv, far_send, far_recv,
):
    sta = lax.axis_index("sta")
    stk = lax.axis_index("stk")
    plan = routes(n_sta)
    hops = sorted({hop for _, _, hop in plan})
    sources = (x_ref, mask_ref, first_ref, twist_ref, last_ref)
    targets = (x_here, masks, first_here, twist_out, last_here)
    loads = [
        pltpu.make_async_copy(source, target, load_sem.at[index])
        for index, (source, target) in enumerate(zip(sources, targets))
    ]
    for load in loads:
        load.start()
    barrier = pltpu.get_barrier_semaphore()
    for hop in hops:
        pl.semaphore_signal(
            barrier, inc=1, device_id=(jnp.bitwise_xor(sta, hop), stk), device_id_type=MESH
        )
    for other in range(1, n_stk):
        pl.semaphore_signal(
            barrier, inc=1, device_id=(sta, jnp.bitwise_xor(stk, other)), device_id_type=MESH
        )

    loads[0].wait()
    _, stations, _, bins = x_here.shape
    rows = bins // LANES
    for s in range(stations):
        for a in range(rows):
            stage[s, :, a, :] = x_here[0, s, :, a * LANES : (a + 1) * LANES]
    for s in range(stations):
        re = stage[s, 0]
        im = stage[s, 1]
        power = re * re + im * im
        level = jnp.sum(power, keepdims=True) * (1.0 / bins)
        denom = jnp.sqrt(power + 0.05 * (level + 1e-06))
        slots[0, s, 0] = (re / denom).astype(jnp.bfloat16)
        slots[0, s, 1] = (im / denom).astype(jnp.bfloat16)

    pl.semaphore_wait(barrier, len(hops) + n_stk - 1)

    def link(d, parent, hop):
        return pltpu.make_async_remote_copy(
            src_ref=slots.at[parent],
            dst_ref=slots.at[d],
            send_sem=send_sem.at[d],
            recv_sem=recv_sem.at[d],
            device_id=(jnp.bitwise_xor(sta, hop), stk),
            device_id_type=MESH,
        )

    copies = {d: link(d, parent, hop) for d, parent, hop in plan}
    children = {}
    for d, parent, _ in plan:
        children.setdefault(parent, []).append(d)
    for d in children[0]:
        copies[d].start()

    own_ref[stk] = slots[0]
    own_copies = []
    for other in range(1, n_stk):
        peer = (sta, jnp.bitwise_xor(stk, other))
        copy = pltpu.make_async_remote_copy(
            src_ref=slots.at[0],
            dst_ref=own_ref.at[stk],
            send_sem=own_send.at[other],
            recv_sem=own_recv.at[other],
            device_id=peer,
            device_id_type=MESH,
        )
        copy.start()
        own_copies.append(copy)

    for load in loads[1:]:
        load.wait()
    first_out[...] = first_here[...].astype(jnp.bfloat16)
    last_out[...] = last_here[...].astype(jnp.bfloat16)

    for d, _, _ in plan:
        copies[d].wait_recv()
        for child in children.get(d, []):
            copies[child].start()

    far_copies = []
    for r in range(far_ref.shape[1]):
        far_ref[stk, r] = slots[masks[r]]
    for other in range(1, n_stk):
        copy = pltpu.make_async_remote_copy(
            src_ref=far_ref.at[stk],
            dst_ref=far_ref.at[stk],
            send_sem=far_send.at[other],
            recv_sem=far_recv.at[other],
            device_id=(sta, jnp.bitwise_xor(stk, other)),
            device_id_type=MESH,
        )
        copy.start()
        far_copies.append(copy)
    for d, _, _ in plan:
        copies[d].wait_send()
    for copy in own_copies + far_copies:
        copy.wait()


def split(value):
    high = value.astype(jnp.bfloat16)
    low = (value - high.astype(jnp.float32)).astype(jnp.bfloat16)
    return high, low


def transform_kernel(
    n_stk, own_ref, far_ref, first_ref, twist_ref, last_ref, out_ref, joined, turned, lagged
):
    stk = lax.axis_index("stk")
    pairs, rounds, lags = out_ref.shape
    stations = far_ref.shape[2]
    grid = far_ref.shape[4:]
    rows = grid[0]
    bin_index = LANES * lax.broadcasted_iota(jnp.int32, grid, 0) + lax.broadcasted_iota(
        jnp.int32, grid, 1
    )
    weight = jnp.where(bin_index == 0, 0.5, 1.0).astype(jnp.float32)
    lane = lax.broadcasted_iota(jnp.int32, (GROUP_ROWS, LANES), 1)
    for p in range(pairs):
        pair = stk * pairs + p
        i = pair // stations
        j = lax.rem(pair, stations)
        own = [
            [own_ref[w, i, c].astype(jnp.float32) * weight for c in range(2)]
            for w in range(n_stk)
        ]
        for r in range(rounds):
            re = im = None
            for w in range(n_stk):
                ar, ai = own[w]
                br = far_ref[w, r, j, 0].astype(jnp.float32)
                bi = far_ref[w, r, j, 1].astype(jnp.float32)
                re_w = ar * br + ai * bi
                im_w = ai * br - ar * bi
                re = re_w if re is None else re + re_w
                im = im_w if im is None else im + im_w
            re_high, re_low = split(re)
            im_high, im_low = split(im)
            parts = (re_high, im_high, re_low, im_low, re_high, im_high)
            for index, part in enumerate(parts):
                joined[
                    p, index * rows : (index + 1) * rows, r * LANES : (r + 1) * LANES
                ] = part
    for p in range(pairs):
        inner = jnp.dot(first_ref[...], joined[p], preferred_element_type=jnp.float32)
        for r in range(rounds):
            in_re = inner[:FINE, r * LANES : (r + 1) * LANES]
            in_im = inner[FINE:, r * LANES : (r + 1) * LANES]
            here = slice(r * FINE, (r + 1) * FINE)
            for c, value in enumerate(
                (
                    in_re * twist_ref[0] - in_im * twist_ref[1],
                    in_re * twist_ref[1] + in_im * twist_ref[0],
                )
            ):
                high, low = split(value)
                turned[0, p, here, c * LANES : (c + 1) * LANES] = high
                turned[1, p, here, c * LANES : (c + 1) * LANES] = low
    contract = (((1,), (1,)), ((), ()))
    for p in range(pairs):
        both = lax.dot_general(
            last_ref[...], turned[0, p], contract, preferred_element_type=jnp.float32
        )
        rest = lax.dot_general(
            last_ref[: 2 * GROUP_ROWS], turned[1, p], contract,
            preferred_element_type=jnp.float32,
        )
        series = both[: 2 * GROUP_ROWS] + both[2 * GROUP_ROWS :] + rest
        for half in range(rounds // 2):
            even = series[:GROUP_ROWS, half * LANES : (half + 1) * LANES]
            odd = series[GROUP_ROWS:, half * LANES : (half + 1) * LANES]
            base = (p * rounds + 2 * half) * GROUP_ROWS
            lagged[base : base + GROUP_ROWS] = jnp.where(lane < FINE, even, pltpu.roll(odd, FINE, 1))
            lagged[base + GROUP_ROWS : base + 2 * GROUP_ROWS] = jnp.where(
                lane < FINE, pltpu.roll(even, FINE, 1), odd
            )
    for p in range(pairs):
        for g in range(GROUPS):
            span = min(LANES, lags - g * LANES)
            values = lagged[pl.ds(p * rounds * GROUP_ROWS + g, rounds, stride=GROUP_ROWS), :]
            out_ref[p, :, g * LANES : g * LANES + span] = values[:, :span]


def turn(product):
    return np.remainder(product, NFFT) * (2.0 * math.pi / NFFT)


def tables(bins, windows):
    a = np.arange(bins // LANES)
    f = np.arange(FINE)
    c = np.arange(LANES)
    scale = 2.0 / math.sqrt(windows * bins)
    angle = turn(LANES * a[None, :] * (f[:, None] - MAXLAG))
    cos, sin = np.cos(angle), np.sin(angle)
    first = np.block([[cos, -sin], [sin, cos]]).astype(np.float32)
    angle = turn(c[None, :] * (f[:, None] - MAXLAG))
    twist = (np.stack([np.cos(angle), np.sin(angle)]) * scale).astype(np.float32)
    group = np.zeros((2, GROUP_ROWS), np.int64)
    group[0, :GROUPS] = 2 * np.arange(GROUPS)
    group[1, :GROUPS] = 2 * np.arange(GROUPS) + 1
    angle = turn(FINE * group.reshape(-1)[:, None] * c[None, :])
    last = np.concatenate([np.cos(angle), -np.sin(angle)], axis=1).astype(np.float32)

    def halves(table):
        high = table.astype(ml_dtypes.bfloat16).astype(np.float32)
        return high, (table - high).astype(ml_dtypes.bfloat16).astype(np.float32)

    first_high, first_low = halves(first)
    last_high, last_low = halves(last)
    return (
        np.concatenate([first_high, first_high, first_low], axis=1),
        twist,
        np.concatenate([last_high, last_low], axis=0),
    )


def body(n_sta, n_stk, spectra, partner_masks):
    _, stations, parts, bins = spectra.shape
    rounds = partner_masks.shape[0]
    rows = bins // LANES
    block = (stations, parts, rows, LANES)
    fixed = tables(bins, n_stk)
    first_shape, twist_shape, last_shape = [table.shape for table in fixed]
    operands = [
        pltpu.with_memory_space_constraint(jnp.asarray(operand), pltpu.HBM)
        for operand in (spectra, partner_masks, *fixed)
    ]
    own, far, first, twist, last = pl.pallas_call(
        functools.partial(gather_kernel, n_sta, n_stk),
        out_shape=[
            jax.ShapeDtypeStruct((n_stk,) + block, jnp.bfloat16),
            jax.ShapeDtypeStruct((n_stk, rounds) + block, jnp.bfloat16),
            jax.ShapeDtypeStruct(first_shape, jnp.bfloat16),
            jax.ShapeDtypeStruct(twist_shape, jnp.float32),
            jax.ShapeDtypeStruct(last_shape, jnp.bfloat16),
        ],
        in_specs=[pl.BlockSpec(memory_space=pltpu.HBM)] * 5,
        out_specs=[VMEM] * 5,
        scratch_shapes=[
            pltpu.VMEM(spectra.shape, jnp.float32),
            pltpu.SMEM((rounds,), jnp.int32),
            pltpu.VMEM(first_shape, jnp.float32),
            pltpu.VMEM(last_shape, jnp.float32),
            pltpu.VMEM(block, jnp.float32),
            pltpu.VMEM((n_sta,) + block, jnp.bfloat16),
            pltpu.SemaphoreType.DMA((5,)),
            pltpu.SemaphoreType.DMA((n_sta,)),
            pltpu.SemaphoreType.DMA((n_sta,)),
            pltpu.SemaphoreType.DMA((n_stk,)),
            pltpu.SemaphoreType.DMA((n_stk,)),
            pltpu.SemaphoreType.DMA((n_stk,)),
            pltpu.SemaphoreType.DMA((n_stk,)),
        ],
        compiler_params=pltpu.CompilerParams(
            collective_id=0, has_side_effects=True, vmem_limit_bytes=32 * 2**20
        ),
        name="whiten_gather",
    )(*operands)
    pairs = stations * stations // n_stk
    return pl.pallas_call(
        functools.partial(transform_kernel, n_stk),
        out_shape=jax.ShapeDtypeStruct((pairs, rounds, 2 * MAXLAG), jnp.float32),
        in_specs=[VMEM] * 5,
        out_specs=VMEM,
        scratch_shapes=[
            pltpu.VMEM((pairs, 6 * rows, rounds * LANES), jnp.bfloat16),
            pltpu.VMEM((2, pairs, rounds * FINE, 2 * LANES), jnp.bfloat16),
            pltpu.VMEM((pairs * rounds * GROUP_ROWS, LANES), jnp.float32),
        ],
        compiler_params=pltpu.CompilerParams(vmem_limit_bytes=32 * 2**20),
        name="cross_transform",
    )(own, far, first, twist, last)


def solution(mesh):
    return jax.shard_map(
        functools.partial(body, mesh.shape["sta"], mesh.shape["stk"]),
        mesh=mesh,
        in_specs=(P("stk", "sta", None, None), P()),
        out_specs=P(("sta", "stk"), None, None),
        check_vma=False,
    )
```

```python
import functools
import math

import jax
import jax.numpy as jnp
import ml_dtypes
import numpy as np
from jax import lax
from jax.experimental import pallas as pl
from jax.experimental.pallas import tpu as pltpu
from jax.sharding import PartitionSpec as P

NFFT = 8192
MAXLAG = 1200
LANES = 128
FINE = NFFT // LANES
GROUPS = -(-2 * MAXLAG // LANES)
GROUP_ROWS = -(-GROUPS // 8) * 8
MESH = pl.DeviceIdType.MESH
VMEM = pl.BlockSpec(memory_space=pltpu.VMEM)


def routes(count):
    plan = [(high, 0, high) for high in reversed(range(4, count, 4))]
    plan += [(low, 0, low) for low in (1, 2, 3)]
    plan += [(high | low, high, low) for high in range(8, count, 4) for low in (1, 2, 3)]
    plan += [(4 | low, low, 4) for low in (1, 2, 3)]
    return plan


def gather_kernel(
    n_sta, n_stk, x_ref, mask_ref, first_ref, twist_ref, last_ref,
    own_ref, far_ref, first_out, twist_out, last_out,
    x_here, masks, first_here, last_here, stage, slots, load_sem,
    send_sem, recv_sem, own_send, own_recv, far_send, far_recv,
):
    sta = lax.axis_index("sta")
    stk = lax.axis_index("stk")
    plan = routes(n_sta)
    hops = sorted({hop for _, _, hop in plan})
    sources = (x_ref, mask_ref, first_ref, twist_ref, last_ref)
    targets = (x_here, masks, first_here, twist_out, last_here)
    loads = [
        pltpu.make_async_copy(source, target, load_sem.at[index])
        for index, (source, target) in enumerate(zip(sources, targets))
    ]
    for load in loads:
        load.start()
    barrier = pltpu.get_barrier_semaphore()
    for hop in hops:
        pl.semaphore_signal(
            barrier, inc=1, device_id=(jnp.bitwise_xor(sta, hop), stk), device_id_type=MESH
        )
    for other in range(1, n_stk):
        pl.semaphore_signal(
            barrier, inc=1, device_id=(sta, jnp.bitwise_xor(stk, other)), device_id_type=MESH
        )

    loads[0].wait()
    _, stations, _, bins = x_here.shape
    rows = bins // LANES
    for s in range(stations):
        for a in range(rows):
            stage[s, :, a, :] = x_here[0, s, :, a * LANES : (a + 1) * LANES]
    for s in range(stations):
        re = stage[s, 0]
        im = stage[s, 1]
        power = re * re + im * im
        level = jnp.sum(power, keepdims=True) * (1.0 / bins)
        denom = jnp.sqrt(power + 0.05 * (level + 1e-06))
        slots[0, s, 0] = (re / denom).astype(jnp.bfloat16)
        slots[0, s, 1] = (im / denom).astype(jnp.bfloat16)

    pl.semaphore_wait(barrier, len(hops) + n_stk - 1)

    def link(d, parent, hop):
        return pltpu.make_async_remote_copy(
            src_ref=slots.at[parent],
            dst_ref=slots.at[d],
            send_sem=send_sem.at[d],
            recv_sem=recv_sem.at[d],
            device_id=(jnp.bitwise_xor(sta, hop), stk),
            device_id_type=MESH,
        )

    copies = {d: link(d, parent, hop) for d, parent, hop in plan}
    children = {}
    for d, parent, _ in plan:
        children.setdefault(parent, []).append(d)
    for d in children[0]:
        copies[d].start()

    own_ref[stk] = slots[0]
    own_copies = []
    for other in range(1, n_stk):
        peer = (sta, jnp.bitwise_xor(stk, other))
        copy = pltpu.make_async_remote_copy(
            src_ref=slots.at[0],
            dst_ref=own_ref.at[stk],
            send_sem=own_send.at[other],
            recv_sem=own_recv.at[other],
            device_id=peer,
            device_id_type=MESH,
        )
        copy.start()
        own_copies.append(copy)

    for load in loads[1:]:
        load.wait()
    first_out[...] = first_here[...].astype(jnp.bfloat16)
    last_out[...] = last_here[...].astype(jnp.bfloat16)

    for d, _, _ in plan:
        copies[d].wait_recv()
        for child in children.get(d, []):
            copies[child].start()

    far_copies = []
    for r in range(far_ref.shape[1]):
        far_ref[stk, r] = slots[masks[r]]
        for other in range(1, n_stk):
            copy = pltpu.make_async_remote_copy(
                src_ref=far_ref.at[stk, r],
                dst_ref=far_ref.at[stk, r],
                send_sem=far_send.at[r, other],
                recv_sem=far_recv.at[r, other],
                device_id=(sta, jnp.bitwise_xor(stk, other)),
                device_id_type=MESH,
            )
            copy.start()
            far_copies.append(copy)
    for d, _, _ in plan:
        copies[d].wait_send()
    for copy in own_copies + far_copies:
        copy.wait()


def split(value):
    high = value.astype(jnp.bfloat16)
    low = (value - high.astype(jnp.float32)).astype(jnp.bfloat16)
    return high, low


def transform_kernel(
    n_stk, own_ref, far_ref, first_ref, twist_ref, last_ref, out_ref, joined, turned, lagged
):
    stk = lax.axis_index("stk")
    pairs, rounds, lags = out_ref.shape
    stations = far_ref.shape[2]
    grid = far_ref.shape[4:]
    rows = grid[0]
    bin_index = LANES * lax.broadcasted_iota(jnp.int32, grid, 0) + lax.broadcasted_iota(
        jnp.int32, grid, 1
    )
    weight = jnp.where(bin_index == 0, 0.5, 1.0).astype(jnp.float32)
    lane = lax.broadcasted_iota(jnp.int32, (GROUP_ROWS, LANES), 1)
    for p in range(pairs):
        pair = stk * pairs + p
        i = pair // stations
        j = lax.rem(pair, stations)
        own = [
            [own_ref[w, i, c].astype(jnp.float32) * weight for c in range(2)]
            for w in range(n_stk)
        ]
        for r in range(rounds):
            re = im = None
            for w in range(n_stk):
                ar, ai = own[w]
                br = far_ref[w, r, j, 0].astype(jnp.float32)
                bi = far_ref[w, r, j, 1].astype(jnp.float32)
                re_w = ar * br + ai * bi
                im_w = ai * br - ar * bi
                re = re_w if re is None else re + re_w
                im = im_w if im is None else im + im_w
            re_high, re_low = split(re)
            im_high, im_low = split(im)
            parts = (re_high, im_high, re_low, im_low, re_high, im_high)
            for index, part in enumerate(parts):
                joined[
                    p, index * rows : (index + 1) * rows, r * LANES : (r + 1) * LANES
                ] = part
    for p in range(pairs):
        inner = jnp.dot(first_ref[...], joined[p], preferred_element_type=jnp.float32)
        for r in range(rounds):
            in_re = inner[:FINE, r * LANES : (r + 1) * LANES]
            in_im = inner[FINE:, r * LANES : (r + 1) * LANES]
            here = slice(r * FINE, (r + 1) * FINE)
            for c, value in enumerate(
                (
                    in_re * twist_ref[0] - in_im * twist_ref[1],
                    in_re * twist_ref[1] + in_im * twist_ref[0],
                )
            ):
                turned[p, here, c * LANES : (c + 1) * LANES] = value.astype(jnp.bfloat16)
    contract = (((1,), (1,)), ((), ()))
    for p in range(pairs):
        both = lax.dot_general(
            last_ref[...], turned[p], contract, preferred_element_type=jnp.float32
        )
        series = both[: 2 * GROUP_ROWS] + both[2 * GROUP_ROWS :]
        for half in range(rounds // 2):
            even = series[:GROUP_ROWS, half * LANES : (half + 1) * LANES]
            odd = series[GROUP_ROWS:, half * LANES : (half + 1) * LANES]
            base = (p * rounds + 2 * half) * GROUP_ROWS
            lagged[base : base + GROUP_ROWS] = jnp.where(lane < FINE, even, pltpu.roll(odd, FINE, 1))
            lagged[base + GROUP_ROWS : base + 2 * GROUP_ROWS] = jnp.where(
                lane < FINE, pltpu.roll(even, FINE, 1), odd
            )
    for p in range(pairs):
        for g in range(GROUPS):
            span = min(LANES, lags - g * LANES)
            values = lagged[pl.ds(p * rounds * GROUP_ROWS + g, rounds, stride=GROUP_ROWS), :]
            out_ref[p, :, g * LANES : g * LANES + span] = values[:, :span]


def turn(product):
    return np.remainder(product, NFFT) * (2.0 * math.pi / NFFT)


def tables(bins, windows):
    a = np.arange(bins // LANES)
    f = np.arange(FINE)
    c = np.arange(LANES)
    scale = 2.0 / math.sqrt(windows * bins)
    angle = turn(LANES * a[None, :] * (f[:, None] - MAXLAG))
    cos, sin = np.cos(angle), np.sin(angle)
    first = np.block([[cos, -sin], [sin, cos]]).astype(np.float32)
    angle = turn(c[None, :] * (f[:, None] - MAXLAG))
    twist = (np.stack([np.cos(angle), np.sin(angle)]) * scale).astype(np.float32)
    group = np.zeros((2, GROUP_ROWS), np.int64)
    group[0, :GROUPS] = 2 * np.arange(GROUPS)
    group[1, :GROUPS] = 2 * np.arange(GROUPS) + 1
    angle = turn(FINE * group.reshape(-1)[:, None] * c[None, :])
    last = np.concatenate([np.cos(angle), -np.sin(angle)], axis=1).astype(np.float32)

    def halves(table):
        high = table.astype(ml_dtypes.bfloat16).astype(np.float32)
        return high, (table - high).astype(ml_dtypes.bfloat16).astype(np.float32)

    first_high, first_low = halves(first)
    last_high, last_low = halves(last)
    return (
        np.concatenate([first_high, first_high, first_low], axis=1),
        twist,
        np.concatenate([last_high, last_low], axis=0),
    )


def body(n_sta, n_stk, spectra, partner_masks):
    _, stations, parts, bins = spectra.shape
    rounds = partner_masks.shape[0]
    rows = bins // LANES
    block = (stations, parts, rows, LANES)
    fixed = tables(bins, n_stk)
    first_shape, twist_shape, last_shape = [table.shape for table in fixed]
    operands = [
        pltpu.with_memory_space_constraint(jnp.asarray(operand), pltpu.HBM)
        for operand in (spectra, partner_masks, *fixed)
    ]
    own, far, first, twist, last = pl.pallas_call(
        functools.partial(gather_kernel, n_sta, n_stk),
        out_shape=[
            jax.ShapeDtypeStruct((n_stk,) + block, jnp.bfloat16),
            jax.ShapeDtypeStruct((n_stk, rounds) + block, jnp.bfloat16),
            jax.ShapeDtypeStruct(first_shape, jnp.bfloat16),
            jax.ShapeDtypeStruct(twist_shape, jnp.float32),
            jax.ShapeDtypeStruct(last_shape, jnp.bfloat16),
        ],
        in_specs=[pl.BlockSpec(memory_space=pltpu.HBM)] * 5,
        out_specs=[VMEM] * 5,
        scratch_shapes=[
            pltpu.VMEM(spectra.shape, jnp.float32),
            pltpu.SMEM((rounds,), jnp.int32),
            pltpu.VMEM(first_shape, jnp.float32),
            pltpu.VMEM(last_shape, jnp.float32),
            pltpu.VMEM(block, jnp.float32),
            pltpu.VMEM((n_sta,) + block, jnp.bfloat16),
            pltpu.SemaphoreType.DMA((5,)),
            pltpu.SemaphoreType.DMA((n_sta,)),
            pltpu.SemaphoreType.DMA((n_sta,)),
            pltpu.SemaphoreType.DMA((n_stk,)),
            pltpu.SemaphoreType.DMA((n_stk,)),
            pltpu.SemaphoreType.DMA((rounds, n_stk)),
            pltpu.SemaphoreType.DMA((rounds, n_stk)),
        ],
        compiler_params=pltpu.CompilerParams(
            collective_id=0, has_side_effects=True, vmem_limit_bytes=32 * 2**20
        ),
        name="whiten_gather",
    )(*operands)
    pairs = stations * stations // n_stk
    return pl.pallas_call(
        functools.partial(transform_kernel, n_stk),
        out_shape=jax.ShapeDtypeStruct((pairs, rounds, 2 * MAXLAG), jnp.float32),
        in_specs=[VMEM] * 5,
        out_specs=VMEM,
        scratch_shapes=[
            pltpu.VMEM((pairs, 6 * rows, rounds * LANES), jnp.bfloat16),
            pltpu.VMEM((pairs, rounds * FINE, 2 * LANES), jnp.bfloat16),
            pltpu.VMEM((pairs * rounds * GROUP_ROWS, LANES), jnp.float32),
        ],
        compiler_params=pltpu.CompilerParams(vmem_limit_bytes=32 * 2**20),
        name="cross_transform",
    )(own, far, first, twist, last)


def solution(mesh):
    return jax.shard_map(
        functools.partial(body, mesh.shape["sta"], mesh.shape["stk"]),
        mesh=mesh,
        in_specs=(P("stk", "sta", None, None), P()),
        out_specs=P(("sta", "stk"), None, None),
        check_vma=False,
    )
```

```python
import functools
import math

import jax
import jax.numpy as jnp
import ml_dtypes
import numpy as np
from jax import lax
from jax.experimental import pallas as pl
from jax.experimental.pallas import tpu as pltpu
from jax.sharding import PartitionSpec as P

NFFT = 8192
MAXLAG = 1200
LANES = 128
FINE = NFFT // LANES
GROUPS = -(-2 * MAXLAG // LANES)
GROUP_ROWS = -(-GROUPS // 8) * 8
MESH = pl.DeviceIdType.MESH
VMEM = pl.BlockSpec(memory_space=pltpu.VMEM)


def zipped(first, second):
    turns = min(len(first), len(second))
    mixed = [item for pair in zip(first, second) for item in pair]
    return mixed + first[turns:] + second[turns:]


def gather_kernel(
    n_sta, n_stk, x_ref, mask_ref, first_ref, twist_ref, last_ref,
    own_ref, far_ref, first_out, twist_out, last_out,
    x_here, masks, first_here, last_here, stage, slots, load_sem,
    send_sem, recv_sem, own_send, own_recv, far_send, far_recv,
):
    sta = lax.axis_index("sta")
    stk = lax.axis_index("stk")
    core = lax.rem(stk, 2)
    highs = list(range(8, n_sta, 4)) + [4]
    lows = [1, 2, 3]
    hops = highs + lows
    sources = (x_ref, mask_ref, first_ref, twist_ref, last_ref)
    targets = (x_here, masks, first_here, twist_out, last_here)
    loads = [
        pltpu.make_async_copy(source, target, load_sem.at[index])
        for index, (source, target) in enumerate(zip(sources, targets))
    ]
    for load in loads:
        load.start()
    barrier = pltpu.get_barrier_semaphore()
    for hop in hops:
        pl.semaphore_signal(
            barrier, inc=1, device_id=(jnp.bitwise_xor(sta, hop), stk), device_id_type=MESH
        )
    for other in range(1, n_stk):
        pl.semaphore_signal(
            barrier, inc=1, device_id=(sta, jnp.bitwise_xor(stk, other)), device_id_type=MESH
        )

    loads[0].wait()
    _, stations, _, bins = x_here.shape
    rows = bins // LANES
    for s in range(stations):
        for a in range(rows):
            stage[s, :, a, :] = x_here[0, s, :, a * LANES : (a + 1) * LANES]
    for s in range(stations):
        re = stage[s, 0]
        im = stage[s, 1]
        power = re * re + im * im
        level = jnp.sum(power, keepdims=True) * (1.0 / bins)
        denom = jnp.sqrt(power + 0.05 * (level + 1e-06))
        slots[0, s, 0] = (re / denom).astype(jnp.bfloat16)
        slots[0, s, 1] = (im / denom).astype(jnp.bfloat16)

    pl.semaphore_wait(barrier, len(hops) + n_stk - 1)

    def link(d, hop):
        return pltpu.make_async_remote_copy(
            src_ref=slots.at[jnp.bitwise_xor(d, hop)],
            dst_ref=slots.at[d],
            send_sem=send_sem.at[d],
            recv_sem=recv_sem.at[d],
            device_id=(jnp.bitwise_xor(sta, hop), stk),
            device_id_type=MESH,
        )

    def start_in_turns(base, even_order, odd_order):
        for even, odd in zip(even_order, odd_order):
            hop = even + core * (odd - even)
            link(base + hop, hop).start()

    start_in_turns(0, zipped(highs, lows), zipped(lows, highs))

    own_ref[stk] = slots[0]
    own_copies = []
    for other in range(1, n_stk):
        peer = (sta, jnp.bitwise_xor(stk, other))
        copy = pltpu.make_async_remote_copy(
            src_ref=slots.at[0],
            dst_ref=own_ref.at[stk],
            send_sem=own_send.at[other],
            recv_sem=own_recv.at[other],
            device_id=peer,
            device_id_type=MESH,
        )
        copy.start()
        own_copies.append(copy)

    for load in loads[1:]:
        load.wait()
    first_out[...] = first_here[...].astype(jnp.bfloat16)
    last_out[...] = last_here[...].astype(jnp.bfloat16)

    for high in highs[:-1]:
        link(high, high).wait_recv()
        start_in_turns(high, [1, 3, 2], [2, 1, 3])
        if high == 8:
            link(1, 1).wait_recv()
            link(5, 4).start()
    for low in lows:
        if low > 1:
            link(low, low).wait_recv()
            link(4 | low, 4).start()
    link(4, 4).wait_recv()
    for low in lows:
        link(4 | low, 4).wait_recv()
    for high in highs[:-1]:
        for low in lows:
            link(high | low, low).wait_recv()

    far_copies = []
    for r in range(far_ref.shape[1]):
        far_ref[stk, r] = slots[masks[r]]
        for other in range(1, n_stk):
            copy = pltpu.make_async_remote_copy(
                src_ref=far_ref.at[stk, r],
                dst_ref=far_ref.at[stk, r],
                send_sem=far_send.at[r, other],
                recv_sem=far_recv.at[r, other],
                device_id=(sta, jnp.bitwise_xor(stk, other)),
                device_id_type=MESH,
            )
            copy.start()
            far_copies.append(copy)
    for d in range(1, n_sta):
        link(d, d).wait_send()
    for copy in own_copies + far_copies:
        copy.wait()


def split(value):
    high = value.astype(jnp.bfloat16)
    low = (value - high.astype(jnp.float32)).astype(jnp.bfloat16)
    return high, low


def transform_kernel(
    n_stk, own_ref, far_ref, first_ref, twist_ref, last_ref, out_ref, joined, turned, lagged
):
    stk = lax.axis_index("stk")
    pairs, rounds, lags = out_ref.shape
    stations = far_ref.shape[2]
    grid = far_ref.shape[4:]
    rows = grid[0]
    bin_index = LANES * lax.broadcasted_iota(jnp.int32, grid, 0) + lax.broadcasted_iota(
        jnp.int32, grid, 1
    )
    weight = jnp.where(bin_index == 0, 0.5, 1.0).astype(jnp.float32)
    lane = lax.broadcasted_iota(jnp.int32, (GROUP_ROWS, LANES), 1)
    for p in range(pairs):
        pair = stk * pairs + p
        i = pair // stations
        j = lax.rem(pair, stations)
        own = [
            [own_ref[w, i, c].astype(jnp.float32) * weight for c in range(2)]
            for w in range(n_stk)
        ]
        for r in range(rounds):
            re = im = None
            for w in range(n_stk):
                ar, ai = own[w]
                br = far_ref[w, r, j, 0].astype(jnp.float32)
                bi = far_ref[w, r, j, 1].astype(jnp.float32)
                re_w = ar * br + ai * bi
                im_w = ai * br - ar * bi
                re = re_w if re is None else re + re_w
                im = im_w if im is None else im + im_w
            re_high, re_low = split(re)
            im_high, im_low = split(im)
            parts = (re_high, im_high, re_low, im_low, re_high, im_high)
            for index, part in enumerate(parts):
                joined[
                    p, index * rows : (index + 1) * rows, r * LANES : (r + 1) * LANES
                ] = part
    for p in range(pairs):
        inner = jnp.dot(first_ref[...], joined[p], preferred_element_type=jnp.float32)
        for r in range(rounds):
            in_re = inner[:FINE, r * LANES : (r + 1) * LANES]
            in_im = inner[FINE:, r * LANES : (r + 1) * LANES]
            here = slice(r * FINE, (r + 1) * FINE)
            for c, value in enumerate(
                (
                    in_re * twist_ref[0] - in_im * twist_ref[1],
                    in_re * twist_ref[1] + in_im * twist_ref[0],
                )
            ):
                turned[p, here, c * LANES : (c + 1) * LANES] = value.astype(jnp.bfloat16)
    contract = (((1,), (1,)), ((), ()))
    for p in range(pairs):
        both = lax.dot_general(
            last_ref[...], turned[p], contract, preferred_element_type=jnp.float32
        )
        series = both[: 2 * GROUP_ROWS] + both[2 * GROUP_ROWS :]
        for half in range(rounds // 2):
            even = series[:GROUP_ROWS, half * LANES : (half + 1) * LANES]
            odd = series[GROUP_ROWS:, half * LANES : (half + 1) * LANES]
            base = (p * rounds + 2 * half) * GROUP_ROWS
            lagged[base : base + GROUP_ROWS] = jnp.where(lane < FINE, even, pltpu.roll(odd, FINE, 1))
            lagged[base + GROUP_ROWS : base + 2 * GROUP_ROWS] = jnp.where(
                lane < FINE, pltpu.roll(even, FINE, 1), odd
            )
    for p in range(pairs):
        for g in range(GROUPS):
            span = min(LANES, lags - g * LANES)
            values = lagged[pl.ds(p * rounds * GROUP_ROWS + g, rounds, stride=GROUP_ROWS), :]
            out_ref[p, :, g * LANES : g * LANES + span] = values[:, :span]


def turn(product):
    return np.remainder(product, NFFT) * (2.0 * math.pi / NFFT)


def tables(bins, windows):
    a = np.arange(bins // LANES)
    f = np.arange(FINE)
    c = np.arange(LANES)
    scale = 2.0 / math.sqrt(windows * bins)
    angle = turn(LANES * a[None, :] * (f[:, None] - MAXLAG))
    cos, sin = np.cos(angle), np.sin(angle)
    first = np.block([[cos, -sin], [sin, cos]]).astype(np.float32)
    angle = turn(c[None, :] * (f[:, None] - MAXLAG))
    twist = (np.stack([np.cos(angle), np.sin(angle)]) * scale).astype(np.float32)
    group = np.zeros((2, GROUP_ROWS), np.int64)
    group[0, :GROUPS] = 2 * np.arange(GROUPS)
    group[1, :GROUPS] = 2 * np.arange(GROUPS) + 1
    angle = turn(FINE * group.reshape(-1)[:, None] * c[None, :])
    last = np.concatenate([np.cos(angle), -np.sin(angle)], axis=1).astype(np.float32)

    def halves(table):
        high = table.astype(ml_dtypes.bfloat16).astype(np.float32)
        return high, (table - high).astype(ml_dtypes.bfloat16).astype(np.float32)

    first_high, first_low = halves(first)
    last_high, last_low = halves(last)
    return (
        np.concatenate([first_high, first_high, first_low], axis=1),
        twist,
        np.concatenate([last_high, last_low], axis=0),
    )


def body(n_sta, n_stk, spectra, partner_masks):
    _, stations, parts, bins = spectra.shape
    rounds = partner_masks.shape[0]
    rows = bins // LANES
    block = (stations, parts, rows, LANES)
    fixed = tables(bins, n_stk)
    first_shape, twist_shape, last_shape = [table.shape for table in fixed]
    operands = [
        pltpu.with_memory_space_constraint(jnp.asarray(operand), pltpu.HBM)
        for operand in (spectra, partner_masks, *fixed)
    ]
    own, far, first, twist, last = pl.pallas_call(
        functools.partial(gather_kernel, n_sta, n_stk),
        out_shape=[
            jax.ShapeDtypeStruct((n_stk,) + block, jnp.bfloat16),
            jax.ShapeDtypeStruct((n_stk, rounds) + block, jnp.bfloat16),
            jax.ShapeDtypeStruct(first_shape, jnp.bfloat16),
            jax.ShapeDtypeStruct(twist_shape, jnp.float32),
            jax.ShapeDtypeStruct(last_shape, jnp.bfloat16),
        ],
        in_specs=[pl.BlockSpec(memory_space=pltpu.HBM)] * 5,
        out_specs=[VMEM] * 5,
        scratch_shapes=[
            pltpu.VMEM(spectra.shape, jnp.float32),
            pltpu.SMEM((rounds,), jnp.int32),
            pltpu.VMEM(first_shape, jnp.float32),
            pltpu.VMEM(last_shape, jnp.float32),
            pltpu.VMEM(block, jnp.float32),
            pltpu.VMEM((n_sta,) + block, jnp.bfloat16),
            pltpu.SemaphoreType.DMA((5,)),
            pltpu.SemaphoreType.DMA((n_sta,)),
            pltpu.SemaphoreType.DMA((n_sta,)),
            pltpu.SemaphoreType.DMA((n_stk,)),
            pltpu.SemaphoreType.DMA((n_stk,)),
            pltpu.SemaphoreType.DMA((rounds, n_stk)),
            pltpu.SemaphoreType.DMA((rounds, n_stk)),
        ],
        compiler_params=pltpu.CompilerParams(
            collective_id=0, has_side_effects=True, vmem_limit_bytes=32 * 2**20
        ),
        name="whiten_gather",
    )(*operands)
    pairs = stations * stations // n_stk
    return pl.pallas_call(
        functools.partial(transform_kernel, n_stk),
        out_shape=jax.ShapeDtypeStruct((pairs, rounds, 2 * MAXLAG), jnp.float32),
        in_specs=[VMEM] * 5,
        out_specs=VMEM,
        scratch_shapes=[
            pltpu.VMEM((pairs, 6 * rows, rounds * LANES), jnp.bfloat16),
            pltpu.VMEM((pairs, rounds * FINE, 2 * LANES), jnp.bfloat16),
            pltpu.VMEM((pairs * rounds * GROUP_ROWS, LANES), jnp.float32),
        ],
        compiler_params=pltpu.CompilerParams(vmem_limit_bytes=32 * 2**20),
        name="cross_transform",
    )(own, far, first, twist, last)


def solution(mesh):
    return jax.shard_map(
        functools.partial(body, mesh.shape["sta"], mesh.shape["stk"]),
        mesh=mesh,
        in_specs=(P("stk", "sta", None, None), P()),
        out_specs=P(("sta", "stk"), None, None),
        check_vma=False,
    )
```

```python
import functools
import math

import jax
import jax.numpy as jnp
import ml_dtypes
import numpy as np
from jax import lax
from jax.experimental import pallas as pl
from jax.experimental.pallas import tpu as pltpu
from jax.sharding import PartitionSpec as P

NFFT = 8192
MAXLAG = 1200
LANES = 128
FINE = NFFT // LANES
GROUPS = -(-2 * MAXLAG // LANES)
GROUP_ROWS = -(-GROUPS // 8) * 8
MESH = pl.DeviceIdType.MESH
VMEM = pl.BlockSpec(memory_space=pltpu.VMEM)


def gather_kernel(
    n_sta, n_stk, x_ref, mask_ref, first_ref, twist_ref, last_ref,
    own_ref, far_ref, first_out, twist_out, last_out,
    x_here, masks, first_here, last_here, stage, slots, load_sem,
    send_sem, recv_sem, own_send, own_recv, far_send, far_recv,
):
    sta = lax.axis_index("sta")
    stk = lax.axis_index("stk")
    tops = n_sta // 4
    hops = [4 * top for top in range(1, tops)] + [1, 2, 3]
    sources = (x_ref, mask_ref, first_ref, twist_ref, last_ref)
    targets = (x_here, masks, first_here, twist_out, last_here)
    loads = [
        pltpu.make_async_copy(source, target, load_sem.at[index])
        for index, (source, target) in enumerate(zip(sources, targets))
    ]
    for load in loads:
        load.start()
    barrier = pltpu.get_barrier_semaphore()
    for hop in hops:
        pl.semaphore_signal(
            barrier, inc=1, device_id=(jnp.bitwise_xor(sta, hop), stk), device_id_type=MESH
        )
    for other in range(1, n_stk):
        pl.semaphore_signal(
            barrier, inc=1, device_id=(sta, jnp.bitwise_xor(stk, other)), device_id_type=MESH
        )

    loads[0].wait()
    _, stations, _, bins = x_here.shape
    rows = bins // LANES
    for s in range(stations):
        for a in range(rows):
            stage[s, :, a, :] = x_here[0, s, :, a * LANES : (a + 1) * LANES]
    for s in range(stations):
        re = stage[s, 0]
        im = stage[s, 1]
        power = re * re + im * im
        level = jnp.sum(power, keepdims=True) * (1.0 / bins)
        denom = jnp.sqrt(power + 0.05 * (level + 1e-06))
        slots[0, 0, s, 0] = (re / denom).astype(jnp.bfloat16)
        slots[0, 0, s, 1] = (im / denom).astype(jnp.bfloat16)

    pl.semaphore_wait(barrier, len(hops) + n_stk - 1)

    def link(source, target, hop, index):
        return pltpu.make_async_remote_copy(
            src_ref=slots.at[source],
            dst_ref=slots.at[target],
            send_sem=send_sem.at[index],
            recv_sem=recv_sem.at[index],
            device_id=(jnp.bitwise_xor(sta, hop), stk),
            device_id_type=MESH,
        )

    lows = (1, 2, 3)
    to_top = [link((0, 0), (0, top), 4 * top, top) for top in range(1, tops)]
    to_low = [link((0, 0), (low, 0), low, tops + low) for low in lows]
    far_tops = pl.ds(2, tops - 2)
    spread = [link((0, far_tops), (low, far_tops), low, tops + 3 + low) for low in lows]
    side = link((pl.ds(1, 3), 0), (pl.ds(1, 3), 1), 4, 0)
    for copy in to_top[::-1] + to_low:
        copy.start()

    own_ref[stk] = slots[0, 0]
    own_copies = []
    for other in range(1, n_stk):
        peer = (sta, jnp.bitwise_xor(stk, other))
        copy = pltpu.make_async_remote_copy(
            src_ref=slots.at[0, 0],
            dst_ref=own_ref.at[stk],
            send_sem=own_send.at[other],
            recv_sem=own_recv.at[other],
            device_id=peer,
            device_id_type=MESH,
        )
        copy.start()
        own_copies.append(copy)

    for load in loads[1:]:
        load.wait()
    first_out[...] = first_here[...].astype(jnp.bfloat16)
    last_out[...] = last_here[...].astype(jnp.bfloat16)

    for copy in to_top[1:]:
        copy.wait_recv()
    for copy in spread:
        copy.start()
    for copy in to_low:
        copy.wait_recv()
    side.start()
    for copy in [to_top[0], side] + spread:
        copy.wait_recv()

    far_copies = []
    for r in range(far_ref.shape[1]):
        far_ref[stk, r] = slots[jnp.bitwise_and(masks[r], 3), jnp.right_shift(masks[r], 2)]
        for other in range(1, n_stk):
            copy = pltpu.make_async_remote_copy(
                src_ref=far_ref.at[stk, r],
                dst_ref=far_ref.at[stk, r],
                send_sem=far_send.at[r, other],
                recv_sem=far_recv.at[r, other],
                device_id=(sta, jnp.bitwise_xor(stk, other)),
                device_id_type=MESH,
            )
            copy.start()
            far_copies.append(copy)
    for copy in to_top + to_low + spread + [side]:
        copy.wait_send()
    for copy in own_copies + far_copies:
        copy.wait()


def split(value):
    high = value.astype(jnp.bfloat16)
    low = (value - high.astype(jnp.float32)).astype(jnp.bfloat16)
    return high, low


def transform_kernel(
    n_stk, own_ref, far_ref, first_ref, twist_ref, last_ref, out_ref, joined, turned, lagged
):
    stk = lax.axis_index("stk")
    pairs, rounds, lags = out_ref.shape
    stations = far_ref.shape[2]
    grid = far_ref.shape[4:]
    rows = grid[0]
    bin_index = LANES * lax.broadcasted_iota(jnp.int32, grid, 0) + lax.broadcasted_iota(
        jnp.int32, grid, 1
    )
    weight = jnp.where(bin_index == 0, 0.5, 1.0).astype(jnp.float32)
    lane = lax.broadcasted_iota(jnp.int32, (GROUP_ROWS, LANES), 1)
    for p in range(pairs):
        pair = stk * pairs + p
        i = pair // stations
        j = lax.rem(pair, stations)
        own = [
            [own_ref[w, i, c].astype(jnp.float32) * weight for c in range(2)]
            for w in range(n_stk)
        ]
        for r in range(rounds):
            re = im = None
            for w in range(n_stk):
                ar, ai = own[w]
                br = far_ref[w, r, j, 0].astype(jnp.float32)
                bi = far_ref[w, r, j, 1].astype(jnp.float32)
                re_w = ar * br + ai * bi
                im_w = ai * br - ar * bi
                re = re_w if re is None else re + re_w
                im = im_w if im is None else im + im_w
            re_high, re_low = split(re)
            im_high, im_low = split(im)
            parts = (re_high, im_high, re_low, im_low, re_high, im_high)
            for index, part in enumerate(parts):
                joined[
                    p, index * rows : (index + 1) * rows, r * LANES : (r + 1) * LANES
                ] = part
    for p in range(pairs):
        inner = jnp.dot(first_ref[...], joined[p], preferred_element_type=jnp.float32)
        for r in range(rounds):
            in_re = inner[:FINE, r * LANES : (r + 1) * LANES]
            in_im = inner[FINE:, r * LANES : (r + 1) * LANES]
            here = slice(r * FINE, (r + 1) * FINE)
            for c, value in enumerate(
                (
                    in_re * twist_ref[0] - in_im * twist_ref[1],
                    in_re * twist_ref[1] + in_im * twist_ref[0],
                )
            ):
                turned[p, here, c * LANES : (c + 1) * LANES] = value.astype(jnp.bfloat16)
    contract = (((1,), (1,)), ((), ()))
    for p in range(pairs):
        both = lax.dot_general(
            last_ref[...], turned[p], contract, preferred_element_type=jnp.float32
        )
        series = both[: 2 * GROUP_ROWS] + both[2 * GROUP_ROWS :]
        for half in range(rounds // 2):
            even = series[:GROUP_ROWS, half * LANES : (half + 1) * LANES]
            odd = series[GROUP_ROWS:, half * LANES : (half + 1) * LANES]
            base = (p * rounds + 2 * half) * GROUP_ROWS
            lagged[base : base + GROUP_ROWS] = jnp.where(lane < FINE, even, pltpu.roll(odd, FINE, 1))
            lagged[base + GROUP_ROWS : base + 2 * GROUP_ROWS] = jnp.where(
                lane < FINE, pltpu.roll(even, FINE, 1), odd
            )
    for p in range(pairs):
        for g in range(GROUPS):
            span = min(LANES, lags - g * LANES)
            values = lagged[pl.ds(p * rounds * GROUP_ROWS + g, rounds, stride=GROUP_ROWS), :]
            out_ref[p, :, g * LANES : g * LANES + span] = values[:, :span]


def turn(product):
    return np.remainder(product, NFFT) * (2.0 * math.pi / NFFT)


def tables(bins, windows):
    a = np.arange(bins // LANES)
    f = np.arange(FINE)
    c = np.arange(LANES)
    scale = 2.0 / math.sqrt(windows * bins)
    angle = turn(LANES * a[None, :] * (f[:, None] - MAXLAG))
    cos, sin = np.cos(angle), np.sin(angle)
    first = np.block([[cos, -sin], [sin, cos]]).astype(np.float32)
    angle = turn(c[None, :] * (f[:, None] - MAXLAG))
    twist = (np.stack([np.cos(angle), np.sin(angle)]) * scale).astype(np.float32)
    group = np.zeros((2, GROUP_ROWS), np.int64)
    group[0, :GROUPS] = 2 * np.arange(GROUPS)
    group[1, :GROUPS] = 2 * np.arange(GROUPS) + 1
    angle = turn(FINE * group.reshape(-1)[:, None] * c[None, :])
    last = np.concatenate([np.cos(angle), -np.sin(angle)], axis=1).astype(np.float32)

    def halves(table):
        high = table.astype(ml_dtypes.bfloat16).astype(np.float32)
        return high, (table - high).astype(ml_dtypes.bfloat16).astype(np.float32)

    first_high, first_low = halves(first)
    last_high, last_low = halves(last)
    return (
        np.concatenate([first_high, first_high, first_low], axis=1),
        twist,
        np.concatenate([last_high, last_low], axis=0),
    )


def body(n_sta, n_stk, spectra, partner_masks):
    _, stations, parts, bins = spectra.shape
    rounds = partner_masks.shape[0]
    rows = bins // LANES
    block = (stations, parts, rows, LANES)
    fixed = tables(bins, n_stk)
    first_shape, twist_shape, last_shape = [table.shape for table in fixed]
    operands = [
        pltpu.with_memory_space_constraint(jnp.asarray(operand), pltpu.HBM)
        for operand in (spectra, partner_masks, *fixed)
    ]
    own, far, first, twist, last = pl.pallas_call(
        functools.partial(gather_kernel, n_sta, n_stk),
        out_shape=[
            jax.ShapeDtypeStruct((n_stk,) + block, jnp.bfloat16),
            jax.ShapeDtypeStruct((n_stk, rounds) + block, jnp.bfloat16),
            jax.ShapeDtypeStruct(first_shape, jnp.bfloat16),
            jax.ShapeDtypeStruct(twist_shape, jnp.float32),
            jax.ShapeDtypeStruct(last_shape, jnp.bfloat16),
        ],
        in_specs=[pl.BlockSpec(memory_space=pltpu.HBM)] * 5,
        out_specs=[VMEM] * 5,
        scratch_shapes=[
            pltpu.VMEM(spectra.shape, jnp.float32),
            pltpu.SMEM((rounds,), jnp.int32),
            pltpu.VMEM(first_shape, jnp.float32),
            pltpu.VMEM(last_shape, jnp.float32),
            pltpu.VMEM(block, jnp.float32),
            pltpu.VMEM((4, n_sta // 4) + block, jnp.bfloat16),
            pltpu.SemaphoreType.DMA((5,)),
            pltpu.SemaphoreType.DMA((n_sta // 4 + 7,)),
            pltpu.SemaphoreType.DMA((n_sta // 4 + 7,)),
            pltpu.SemaphoreType.DMA((n_stk,)),
            pltpu.SemaphoreType.DMA((n_stk,)),
            pltpu.SemaphoreType.DMA((rounds, n_stk)),
            pltpu.SemaphoreType.DMA((rounds, n_stk)),
        ],
        compiler_params=pltpu.CompilerParams(
            collective_id=0, has_side_effects=True, vmem_limit_bytes=32 * 2**20
        ),
        name="whiten_gather",
    )(*operands)
    pairs = stations * stations // n_stk
    return pl.pallas_call(
        functools.partial(transform_kernel, n_stk),
        out_shape=jax.ShapeDtypeStruct((pairs, rounds, 2 * MAXLAG), jnp.float32),
        in_specs=[VMEM] * 5,
        out_specs=VMEM,
        scratch_shapes=[
            pltpu.VMEM((pairs, 6 * rows, rounds * LANES), jnp.bfloat16),
            pltpu.VMEM((pairs, rounds * FINE, 2 * LANES), jnp.bfloat16),
            pltpu.VMEM((pairs * rounds * GROUP_ROWS, LANES), jnp.float32),
        ],
        compiler_params=pltpu.CompilerParams(vmem_limit_bytes=32 * 2**20),
        name="cross_transform",
    )(own, far, first, twist, last)


def solution(mesh):
    return jax.shard_map(
        functools.partial(body, mesh.shape["sta"], mesh.shape["stk"]),
        mesh=mesh,
        in_specs=(P("stk", "sta", None, None), P()),
        out_specs=P(("sta", "stk"), None, None),
        check_vma=False,
    )
```

```python
import functools
import math

import jax
import jax.numpy as jnp
import ml_dtypes
import numpy as np
from jax import lax
from jax.experimental import pallas as pl
from jax.experimental.pallas import tpu as pltpu
from jax.sharding import PartitionSpec as P

NFFT = 8192
MAXLAG = 1200
LANES = 128
FINE = NFFT // LANES
GROUPS = -(-2 * MAXLAG // LANES)
GROUP_ROWS = -(-GROUPS // 8) * 8
MESH = pl.DeviceIdType.MESH
VMEM = pl.BlockSpec(memory_space=pltpu.VMEM)


def routes(count):
    tops = range(8, count, 8)
    plan = [(top, 0, top) for top in tops]
    plan += [(d, 0, d) for d in (4, 1, 2, 3)]
    plan += [(top | low, top, low) for top in tops for low in (4, 7, 5, 6, 1, 2, 3)]
    plan += [(4 | low, 4, low) for low in (1, 2, 3)]
    return plan


def gather_kernel(
    n_sta, n_stk, x_ref, mask_ref, first_ref, twist_ref, last_ref,
    own_ref, far_ref, first_out, twist_out, last_out,
    x_here, masks, first_here, last_here, stage, slots, load_sem,
    send_sem, recv_sem, own_send, own_recv, far_send, far_recv,
):
    sta = lax.axis_index("sta")
    stk = lax.axis_index("stk")
    plan = routes(n_sta)
    hops = sorted({hop for _, _, hop in plan})
    sources = (x_ref, mask_ref, first_ref, twist_ref, last_ref)
    targets = (x_here, masks, first_here, twist_out, last_here)
    loads = [
        pltpu.make_async_copy(source, target, load_sem.at[index])
        for index, (source, target) in enumerate(zip(sources, targets))
    ]
    for load in loads:
        load.start()
    barrier = pltpu.get_barrier_semaphore()
    for hop in hops:
        pl.semaphore_signal(
            barrier, inc=1, device_id=(jnp.bitwise_xor(sta, hop), stk), device_id_type=MESH
        )
    for other in range(1, n_stk):
        pl.semaphore_signal(
            barrier, inc=1, device_id=(sta, jnp.bitwise_xor(stk, other)), device_id_type=MESH
        )

    loads[0].wait()
    _, stations, _, bins = x_here.shape
    rows = bins // LANES
    for s in range(stations):
        for a in range(rows):
            stage[s, :, a, :] = x_here[0, s, :, a * LANES : (a + 1) * LANES]
    for s in range(stations):
        re = stage[s, 0]
        im = stage[s, 1]
        power = re * re + im * im
        level = jnp.sum(power, keepdims=True) * (1.0 / bins)
        denom = jnp.sqrt(power + 0.05 * (level + 1e-06))
        slots[0, s, 0] = (re / denom).astype(jnp.bfloat16)
        slots[0, s, 1] = (im / denom).astype(jnp.bfloat16)

    pl.semaphore_wait(barrier, len(hops) + n_stk - 1)

    def link(d, parent, hop):
        return pltpu.make_async_remote_copy(
            src_ref=slots.at[parent],
            dst_ref=slots.at[d],
            send_sem=send_sem.at[d],
            recv_sem=recv_sem.at[d],
            device_id=(jnp.bitwise_xor(sta, hop), stk),
            device_id_type=MESH,
        )

    copies = {d: link(d, parent, hop) for d, parent, hop in plan}
    children = {}
    for d, parent, _ in plan:
        children.setdefault(parent, []).append(d)
    for d in children[0]:
        copies[d].start()

    own_ref[stk] = slots[0]
    own_copies = []
    for other in range(1, n_stk):
        peer = (sta, jnp.bitwise_xor(stk, other))
        copy = pltpu.make_async_remote_copy(
            src_ref=slots.at[0],
            dst_ref=own_ref.at[stk],
            send_sem=own_send.at[other],
            recv_sem=own_recv.at[other],
            device_id=peer,
            device_id_type=MESH,
        )
        copy.start()
        own_copies.append(copy)

    for load in loads[1:]:
        load.wait()
    first_out[...] = first_here[...].astype(jnp.bfloat16)
    last_out[...] = last_here[...].astype(jnp.bfloat16)

    for d, _, _ in plan:
        copies[d].wait_recv()
        for child in children.get(d, []):
            copies[child].start()

    far_copies = []
    for r in range(far_ref.shape[1]):
        far_ref[stk, r] = slots[masks[r]]
        for other in range(1, n_stk):
            copy = pltpu.make_async_remote_copy(
                src_ref=far_ref.at[stk, r],
                dst_ref=far_ref.at[stk, r],
                send_sem=far_send.at[r, other],
                recv_sem=far_recv.at[r, other],
                device_id=(sta, jnp.bitwise_xor(stk, other)),
                device_id_type=MESH,
            )
            copy.start()
            far_copies.append(copy)
    for d, _, _ in plan:
        copies[d].wait_send()
    for copy in own_copies + far_copies:
        copy.wait()


def split(value):
    high = value.astype(jnp.bfloat16)
    low = (value - high.astype(jnp.float32)).astype(jnp.bfloat16)
    return high, low


def transform_kernel(
    n_stk, own_ref, far_ref, first_ref, twist_ref, last_ref, out_ref, joined, turned, lagged
):
    stk = lax.axis_index("stk")
    pairs, rounds, lags = out_ref.shape
    stations = far_ref.shape[2]
    grid = far_ref.shape[4:]
    rows = grid[0]
    bin_index = LANES * lax.broadcasted_iota(jnp.int32, grid, 0) + lax.broadcasted_iota(
        jnp.int32, grid, 1
    )
    weight = jnp.where(bin_index == 0, 0.5, 1.0).astype(jnp.float32)
    lane = lax.broadcasted_iota(jnp.int32, (GROUP_ROWS, LANES), 1)
    for p in range(pairs):
        pair = stk * pairs + p
        i = pair // stations
        j = lax.rem(pair, stations)
        own = [
            [own_ref[w, i, c].astype(jnp.float32) * weight for c in range(2)]
            for w in range(n_stk)
        ]
        for r in range(rounds):
            re = im = None
            for w in range(n_stk):
                ar, ai = own[w]
                br = far_ref[w, r, j, 0].astype(jnp.float32)
                bi = far_ref[w, r, j, 1].astype(jnp.float32)
                re_w = ar * br + ai * bi
                im_w = ai * br - ar * bi
                re = re_w if re is None else re + re_w
                im = im_w if im is None else im + im_w
            re_high, re_low = split(re)
            im_high, im_low = split(im)
            parts = (re_high, im_high, re_low, im_low, re_high, im_high)
            for index, part in enumerate(parts):
                joined[
                    p, index * rows : (index + 1) * rows, r * LANES : (r + 1) * LANES
                ] = part
    for p in range(pairs):
        inner = jnp.dot(first_ref[...], joined[p], preferred_element_type=jnp.float32)
        for r in range(rounds):
            in_re = inner[:FINE, r * LANES : (r + 1) * LANES]
            in_im = inner[FINE:, r * LANES : (r + 1) * LANES]
            here = slice(r * FINE, (r + 1) * FINE)
            for c, value in enumerate(
                (
                    in_re * twist_ref[0] - in_im * twist_ref[1],
                    in_re * twist_ref[1] + in_im * twist_ref[0],
                )
            ):
                turned[p, here, c * LANES : (c + 1) * LANES] = value.astype(jnp.bfloat16)
    contract = (((1,), (1,)), ((), ()))
    for p in range(pairs):
        both = lax.dot_general(
            last_ref[...], turned[p], contract, preferred_element_type=jnp.float32
        )
        series = both[: 2 * GROUP_ROWS] + both[2 * GROUP_ROWS :]
        for half in range(rounds // 2):
            even = series[:GROUP_ROWS, half * LANES : (half + 1) * LANES]
            odd = series[GROUP_ROWS:, half * LANES : (half + 1) * LANES]
            base = (p * rounds + 2 * half) * GROUP_ROWS
            lagged[base : base + GROUP_ROWS] = jnp.where(lane < FINE, even, pltpu.roll(odd, FINE, 1))
            lagged[base + GROUP_ROWS : base + 2 * GROUP_ROWS] = jnp.where(
                lane < FINE, pltpu.roll(even, FINE, 1), odd
            )
    for p in range(pairs):
        for g in range(GROUPS):
            span = min(LANES, lags - g * LANES)
            values = lagged[pl.ds(p * rounds * GROUP_ROWS + g, rounds, stride=GROUP_ROWS), :]
            out_ref[p, :, g * LANES : g * LANES + span] = values[:, :span]


def turn(product):
    return np.remainder(product, NFFT) * (2.0 * math.pi / NFFT)


def tables(bins, windows):
    a = np.arange(bins // LANES)
    f = np.arange(FINE)
    c = np.arange(LANES)
    scale = 2.0 / math.sqrt(windows * bins)
    angle = turn(LANES * a[None, :] * (f[:, None] - MAXLAG))
    cos, sin = np.cos(angle), np.sin(angle)
    first = np.block([[cos, -sin], [sin, cos]]).astype(np.float32)
    angle = turn(c[None, :] * (f[:, None] - MAXLAG))
    twist = (np.stack([np.cos(angle), np.sin(angle)]) * scale).astype(np.float32)
    group = np.zeros((2, GROUP_ROWS), np.int64)
    group[0, :GROUPS] = 2 * np.arange(GROUPS)
    group[1, :GROUPS] = 2 * np.arange(GROUPS) + 1
    angle = turn(FINE * group.reshape(-1)[:, None] * c[None, :])
    last = np.concatenate([np.cos(angle), -np.sin(angle)], axis=1).astype(np.float32)

    def halves(table):
        high = table.astype(ml_dtypes.bfloat16).astype(np.float32)
        return high, (table - high).astype(ml_dtypes.bfloat16).astype(np.float32)

    first_high, first_low = halves(first)
    last_high, last_low = halves(last)
    return (
        np.concatenate([first_high, first_high, first_low], axis=1),
        twist,
        np.concatenate([last_high, last_low], axis=0),
    )


def body(n_sta, n_stk, spectra, partner_masks):
    _, stations, parts, bins = spectra.shape
    rounds = partner_masks.shape[0]
    rows = bins // LANES
    block = (stations, parts, rows, LANES)
    fixed = tables(bins, n_stk)
    first_shape, twist_shape, last_shape = [table.shape for table in fixed]
    operands = [
        pltpu.with_memory_space_constraint(jnp.asarray(operand), pltpu.HBM)
        for operand in (spectra, partner_masks, *fixed)
    ]
    own, far, first, twist, last = pl.pallas_call(
        functools.partial(gather_kernel, n_sta, n_stk),
        out_shape=[
            jax.ShapeDtypeStruct((n_stk,) + block, jnp.bfloat16),
            jax.ShapeDtypeStruct((n_stk, rounds) + block, jnp.bfloat16),
            jax.ShapeDtypeStruct(first_shape, jnp.bfloat16),
            jax.ShapeDtypeStruct(twist_shape, jnp.float32),
            jax.ShapeDtypeStruct(last_shape, jnp.bfloat16),
        ],
        in_specs=[pl.BlockSpec(memory_space=pltpu.HBM)] * 5,
        out_specs=[VMEM] * 5,
        scratch_shapes=[
            pltpu.VMEM(spectra.shape, jnp.float32),
            pltpu.SMEM((rounds,), jnp.int32),
            pltpu.VMEM(first_shape, jnp.float32),
            pltpu.VMEM(last_shape, jnp.float32),
            pltpu.VMEM(block, jnp.float32),
            pltpu.VMEM((n_sta,) + block, jnp.bfloat16),
            pltpu.SemaphoreType.DMA((5,)),
            pltpu.SemaphoreType.DMA((n_sta,)),
            pltpu.SemaphoreType.DMA((n_sta,)),
            pltpu.SemaphoreType.DMA((n_stk,)),
            pltpu.SemaphoreType.DMA((n_stk,)),
            pltpu.SemaphoreType.DMA((rounds, n_stk)),
            pltpu.SemaphoreType.DMA((rounds, n_stk)),
        ],
        compiler_params=pltpu.CompilerParams(
            collective_id=0, has_side_effects=True, vmem_limit_bytes=32 * 2**20
        ),
        name="whiten_gather",
    )(*operands)
    pairs = stations * stations // n_stk
    return pl.pallas_call(
        functools.partial(transform_kernel, n_stk),
        out_shape=jax.ShapeDtypeStruct((pairs, rounds, 2 * MAXLAG), jnp.float32),
        in_specs=[VMEM] * 5,
        out_specs=VMEM,
        scratch_shapes=[
            pltpu.VMEM((pairs, 6 * rows, rounds * LANES), jnp.bfloat16),
            pltpu.VMEM((pairs, rounds * FINE, 2 * LANES), jnp.bfloat16),
            pltpu.VMEM((pairs * rounds * GROUP_ROWS, LANES), jnp.float32),
        ],
        compiler_params=pltpu.CompilerParams(vmem_limit_bytes=32 * 2**20),
        name="cross_transform",
    )(own, far, first, twist, last)


def solution(mesh):
    return jax.shard_map(
        functools.partial(body, mesh.shape["sta"], mesh.shape["stk"]),
        mesh=mesh,
        in_specs=(P("stk", "sta", None, None), P()),
        out_specs=P(("sta", "stk"), None, None),
        check_vma=False,
    )
```

```python
import functools
import math

import jax
import jax.numpy as jnp
import ml_dtypes
import numpy as np
from jax import lax
from jax.experimental import pallas as pl
from jax.experimental.pallas import tpu as pltpu
from jax.sharding import PartitionSpec as P

NFFT = 8192
MAXLAG = 1200
LANES = 128
FINE = NFFT // LANES
GROUPS = -(-2 * MAXLAG // LANES)
GROUP_ROWS = -(-GROUPS // 8) * 8
MESH = pl.DeviceIdType.MESH
VMEM = pl.BlockSpec(memory_space=pltpu.VMEM)


def routes(count):
    plan = [(high, 0, high) for high in range(4, count, 4)]
    plan += [(low, 0, low) for low in (1, 2, 3)]
    plan += [(high | low, high, low) for high in range(4, count, 4) for low in (3, 1, 2)]
    return plan


def gather_kernel(
    n_sta, n_stk, x_ref, mask_ref, first_ref, twist_ref, last_ref,
    own_ref, far_ref, first_out, twist_out, last_out,
    x_here, masks, first_here, last_here, stage, slots, load_sem,
    send_sem, recv_sem, own_send, own_recv, far_send, far_recv,
):
    sta = lax.axis_index("sta")
    stk = lax.axis_index("stk")
    plan = routes(n_sta)
    hops = sorted({hop for _, _, hop in plan})
    sources = (x_ref, mask_ref, first_ref, twist_ref, last_ref)
    targets = (x_here, masks, first_here, twist_out, last_here)
    loads = [
        pltpu.make_async_copy(source, target, load_sem.at[index])
        for index, (source, target) in enumerate(zip(sources, targets))
    ]
    for load in loads:
        load.start()
    barrier = pltpu.get_barrier_semaphore()
    for hop in hops:
        pl.semaphore_signal(
            barrier, inc=1, device_id=(jnp.bitwise_xor(sta, hop), stk), device_id_type=MESH
        )
    for other in range(1, n_stk):
        pl.semaphore_signal(
            barrier, inc=1, device_id=(sta, jnp.bitwise_xor(stk, other)), device_id_type=MESH
        )

    loads[0].wait()
    _, stations, _, bins = x_here.shape
    rows = bins // LANES
    for s in range(stations):
        for a in range(rows):
            stage[s, :, a, :] = x_here[0, s, :, a * LANES : (a + 1) * LANES]
    for s in range(stations):
        re = stage[s, 0]
        im = stage[s, 1]
        power = re * re + im * im
        level = jnp.sum(power, keepdims=True) * (1.0 / bins)
        denom = jnp.sqrt(power + 0.05 * (level + 1e-06))
        slots[0, s, 0] = (re / denom).astype(jnp.bfloat16)
        slots[0, s, 1] = (im / denom).astype(jnp.bfloat16)

    pl.semaphore_wait(barrier, len(hops) + n_stk - 1)

    def link(d, parent, hop):
        return pltpu.make_async_remote_copy(
            src_ref=slots.at[parent],
            dst_ref=slots.at[d],
            send_sem=send_sem.at[d],
            recv_sem=recv_sem.at[d],
            device_id=(jnp.bitwise_xor(sta, hop), stk),
            device_id_type=MESH,
        )

    copies = {d: link(d, parent, hop) for d, parent, hop in plan}
    children = {}
    for d, parent, _ in plan:
        children.setdefault(parent, []).append(d)
    for d in sorted(children[0], reverse=True):
        copies[d].start()

    own_ref[stk] = slots[0]
    own_copies = []
    for other in range(1, n_stk):
        peer = (sta, jnp.bitwise_xor(stk, other))
        copy = pltpu.make_async_remote_copy(
            src_ref=slots.at[0],
            dst_ref=own_ref.at[stk],
            send_sem=own_send.at[other],
            recv_sem=own_recv.at[other],
            device_id=peer,
            device_id_type=MESH,
        )
        copy.start()
        own_copies.append(copy)

    for d, _, _ in plan:
        copies[d].wait_recv()
        for child in children.get(d, []):
            copies[child].start()

    loads[1].wait()
    far_copies = []
    for r in range(far_ref.shape[1]):
        far_ref[stk, r] = slots[masks[r]]
        for other in range(1, n_stk):
            copy = pltpu.make_async_remote_copy(
                src_ref=far_ref.at[stk, r],
                dst_ref=far_ref.at[stk, r],
                send_sem=far_send.at[r, other],
                recv_sem=far_recv.at[r, other],
                device_id=(sta, jnp.bitwise_xor(stk, other)),
                device_id_type=MESH,
            )
            copy.start()
            far_copies.append(copy)
    for load in loads[2:]:
        load.wait()
    first_out[...] = first_here[...].astype(jnp.bfloat16)
    last_out[...] = last_here[...].astype(jnp.bfloat16)
    for d, _, _ in plan:
        copies[d].wait_send()
    for copy in own_copies + far_copies:
        copy.wait()


def split(value):
    high = value.astype(jnp.bfloat16)
    low = (value - high.astype(jnp.float32)).astype(jnp.bfloat16)
    return high, low


def transform_kernel(
    n_stk, own_ref, far_ref, first_ref, twist_ref, last_ref, out_ref, joined, turned, lagged
):
    stk = lax.axis_index("stk")
    pairs, rounds, lags = out_ref.shape
    stations = far_ref.shape[2]
    grid = far_ref.shape[4:]
    rows = grid[0]
    bin_index = LANES * lax.broadcasted_iota(jnp.int32, grid, 0) + lax.broadcasted_iota(
        jnp.int32, grid, 1
    )
    weight = jnp.where(bin_index == 0, 0.5, 1.0).astype(jnp.float32)
    lane = lax.broadcasted_iota(jnp.int32, (GROUP_ROWS, LANES), 1)
    for p in range(pairs):
        pair = stk * pairs + p
        i = pair // stations
        j = lax.rem(pair, stations)
        own = [
            [own_ref[w, i, c].astype(jnp.float32) * weight for c in range(2)]
            for w in range(n_stk)
        ]
        for r in range(rounds):
            re = im = None
            for w in range(n_stk):
                ar, ai = own[w]
                br = far_ref[w, r, j, 0].astype(jnp.float32)
                bi = far_ref[w, r, j, 1].astype(jnp.float32)
                re_w = ar * br + ai * bi
                im_w = ai * br - ar * bi
                re = re_w if re is None else re + re_w
                im = im_w if im is None else im + im_w
            re_high, re_low = split(re)
            im_high, im_low = split(im)
            parts = (re_high, im_high, re_low, im_low, re_high, im_high)
            for index, part in enumerate(parts):
                joined[
                    p, index * rows : (index + 1) * rows, r * LANES : (r + 1) * LANES
                ] = part
    for p in range(pairs):
        inner = jnp.dot(first_ref[...], joined[p], preferred_element_type=jnp.float32)
        for r in range(rounds):
            in_re = inner[:FINE, r * LANES : (r + 1) * LANES]
            in_im = inner[FINE:, r * LANES : (r + 1) * LANES]
            here = slice(r * FINE, (r + 1) * FINE)
            for c, value in enumerate(
                (
                    in_re * twist_ref[0] - in_im * twist_ref[1],
                    in_re * twist_ref[1] + in_im * twist_ref[0],
                )
            ):
                turned[p, here, c * LANES : (c + 1) * LANES] = value.astype(jnp.bfloat16)
    contract = (((1,), (1,)), ((), ()))
    for p in range(pairs):
        both = lax.dot_general(
            last_ref[...], turned[p], contract, preferred_element_type=jnp.float32
        )
        series = both[: 2 * GROUP_ROWS] + both[2 * GROUP_ROWS :]
        for half in range(rounds // 2):
            even = series[:GROUP_ROWS, half * LANES : (half + 1) * LANES]
            odd = series[GROUP_ROWS:, half * LANES : (half + 1) * LANES]
            base = (p * rounds + 2 * half) * GROUP_ROWS
            lagged[base : base + GROUP_ROWS] = jnp.where(lane < FINE, even, pltpu.roll(odd, FINE, 1))
            lagged[base + GROUP_ROWS : base + 2 * GROUP_ROWS] = jnp.where(
                lane < FINE, pltpu.roll(even, FINE, 1), odd
            )
    for p in range(pairs):
        for g in range(GROUPS):
            span = min(LANES, lags - g * LANES)
            values = lagged[pl.ds(p * rounds * GROUP_ROWS + g, rounds, stride=GROUP_ROWS), :]
            out_ref[p, :, g * LANES : g * LANES + span] = values[:, :span]


def turn(product):
    return np.remainder(product, NFFT) * (2.0 * math.pi / NFFT)


def tables(bins, windows):
    a = np.arange(bins // LANES)
    f = np.arange(FINE)
    c = np.arange(LANES)
    scale = 2.0 / math.sqrt(windows * bins)
    angle = turn(LANES * a[None, :] * (f[:, None] - MAXLAG))
    cos, sin = np.cos(angle), np.sin(angle)
    first = np.block([[cos, -sin], [sin, cos]]).astype(np.float32)
    angle = turn(c[None, :] * (f[:, None] - MAXLAG))
    twist = (np.stack([np.cos(angle), np.sin(angle)]) * scale).astype(np.float32)
    group = np.zeros((2, GROUP_ROWS), np.int64)
    group[0, :GROUPS] = 2 * np.arange(GROUPS)
    group[1, :GROUPS] = 2 * np.arange(GROUPS) + 1
    angle = turn(FINE * group.reshape(-1)[:, None] * c[None, :])
    last = np.concatenate([np.cos(angle), -np.sin(angle)], axis=1).astype(np.float32)

    def halves(table):
        high = table.astype(ml_dtypes.bfloat16).astype(np.float32)
        return high, (table - high).astype(ml_dtypes.bfloat16).astype(np.float32)

    first_high, first_low = halves(first)
    last_high, last_low = halves(last)
    return (
        np.concatenate([first_high, first_high, first_low], axis=1),
        twist,
        np.concatenate([last_high, last_low], axis=0),
    )


def body(n_sta, n_stk, spectra, partner_masks):
    _, stations, parts, bins = spectra.shape
    rounds = partner_masks.shape[0]
    rows = bins // LANES
    block = (stations, parts, rows, LANES)
    fixed = tables(bins, n_stk)
    first_shape, twist_shape, last_shape = [table.shape for table in fixed]
    operands = [
        pltpu.with_memory_space_constraint(jnp.asarray(operand), pltpu.HBM)
        for operand in (spectra, partner_masks, *fixed)
    ]
    own, far, first, twist, last = pl.pallas_call(
        functools.partial(gather_kernel, n_sta, n_stk),
        out_shape=[
            jax.ShapeDtypeStruct((n_stk,) + block, jnp.bfloat16),
            jax.ShapeDtypeStruct((n_stk, rounds) + block, jnp.bfloat16),
            jax.ShapeDtypeStruct(first_shape, jnp.bfloat16),
            jax.ShapeDtypeStruct(twist_shape, jnp.float32),
            jax.ShapeDtypeStruct(last_shape, jnp.bfloat16),
        ],
        in_specs=[pl.BlockSpec(memory_space=pltpu.HBM)] * 5,
        out_specs=[VMEM] * 5,
        scratch_shapes=[
            pltpu.VMEM(spectra.shape, jnp.float32),
            pltpu.SMEM((rounds,), jnp.int32),
            pltpu.VMEM(first_shape, jnp.float32),
            pltpu.VMEM(last_shape, jnp.float32),
            pltpu.VMEM(block, jnp.float32),
            pltpu.VMEM((n_sta,) + block, jnp.bfloat16),
            pltpu.SemaphoreType.DMA((5,)),
            pltpu.SemaphoreType.DMA((n_sta,)),
            pltpu.SemaphoreType.DMA((n_sta,)),
            pltpu.SemaphoreType.DMA((n_stk,)),
            pltpu.SemaphoreType.DMA((n_stk,)),
            pltpu.SemaphoreType.DMA((rounds, n_stk)),
            pltpu.SemaphoreType.DMA((rounds, n_stk)),
        ],
        compiler_params=pltpu.CompilerParams(
            collective_id=0, has_side_effects=True, vmem_limit_bytes=32 * 2**20
        ),
        name="whiten_gather",
    )(*operands)
    pairs = stations * stations // n_stk
    return pl.pallas_call(
        functools.partial(transform_kernel, n_stk),
        out_shape=jax.ShapeDtypeStruct((pairs, rounds, 2 * MAXLAG), jnp.float32),
        in_specs=[VMEM] * 5,
        out_specs=VMEM,
        scratch_shapes=[
            pltpu.VMEM((pairs, 6 * rows, rounds * LANES), jnp.bfloat16),
            pltpu.VMEM((pairs, rounds * FINE, 2 * LANES), jnp.bfloat16),
            pltpu.VMEM((pairs * rounds * GROUP_ROWS, LANES), jnp.float32),
        ],
        compiler_params=pltpu.CompilerParams(vmem_limit_bytes=32 * 2**20),
        name="cross_transform",
    )(own, far, first, twist, last)


def solution(mesh):
    return jax.shard_map(
        functools.partial(body, mesh.shape["sta"], mesh.shape["stk"]),
        mesh=mesh,
        in_specs=(P("stk", "sta", None, None), P()),
        out_specs=P(("sta", "stk"), None, None),
        check_vma=False,
    )
```

```python
import functools
import math

import jax
import jax.numpy as jnp
import ml_dtypes
import numpy as np
from jax import lax
from jax.experimental import pallas as pl
from jax.experimental.pallas import tpu as pltpu
from jax.sharding import PartitionSpec as P

NFFT = 8192
MAXLAG = 1200
LANES = 128
FINE = NFFT // LANES
GROUPS = -(-2 * MAXLAG // LANES)
GROUP_ROWS = -(-GROUPS // 8) * 8
MESH = pl.DeviceIdType.MESH
VMEM = pl.BlockSpec(memory_space=pltpu.VMEM)


def routes(count):
    highs = range(8, count, 4)
    plan = [(high, 0, high) for high in highs] + [(1, 0, 1), (2, 0, 2)]
    plan += [(9, 8, 1), (3, 2, 1), (4, 0, 4), (5, 1, 4), (6, 2, 4), (7, 3, 4), (10, 8, 2), (11, 9, 2)]
    plan += [(high | low, high, low) for high in highs[1:] for low in (3, 1, 2)]
    return plan


def gather_kernel(
    n_sta, n_stk, x_ref, mask_ref, first_ref, twist_ref, last_ref,
    own_ref, far_ref, first_out, twist_out, last_out,
    x_here, masks, first_here, last_here, stage, slots, load_sem,
    send_sem, recv_sem, own_send, own_recv, far_send, far_recv,
):
    sta = lax.axis_index("sta")
    stk = lax.axis_index("stk")
    plan = routes(n_sta)
    hops = sorted({hop for _, _, hop in plan})
    sources = (x_ref, mask_ref, first_ref, twist_ref, last_ref)
    targets = (x_here, masks, first_here, twist_out, last_here)
    loads = [
        pltpu.make_async_copy(source, target, load_sem.at[index])
        for index, (source, target) in enumerate(zip(sources, targets))
    ]
    for load in loads:
        load.start()
    barrier = pltpu.get_barrier_semaphore()
    for hop in hops:
        pl.semaphore_signal(
            barrier, inc=1, device_id=(jnp.bitwise_xor(sta, hop), stk), device_id_type=MESH
        )
    for other in range(1, n_stk):
        pl.semaphore_signal(
            barrier, inc=1, device_id=(sta, jnp.bitwise_xor(stk, other)), device_id_type=MESH
        )

    loads[0].wait()
    _, stations, _, bins = x_here.shape
    rows = bins // LANES
    for s in range(stations):
        for a in range(rows):
            stage[s, :, a, :] = x_here[0, s, :, a * LANES : (a + 1) * LANES]
    for s in range(stations):
        re = stage[s, 0]
        im = stage[s, 1]
        power = re * re + im * im
        level = jnp.sum(power, keepdims=True) * (1.0 / bins)
        denom = jnp.sqrt(power + 0.05 * (level + 1e-06))
        slots[0, s, 0] = (re / denom).astype(jnp.bfloat16)
        slots[0, s, 1] = (im / denom).astype(jnp.bfloat16)

    pl.semaphore_wait(barrier, len(hops) + n_stk - 1)

    def link(d, parent, hop):
        return pltpu.make_async_remote_copy(
            src_ref=slots.at[parent],
            dst_ref=slots.at[d],
            send_sem=send_sem.at[d],
            recv_sem=recv_sem.at[d],
            device_id=(jnp.bitwise_xor(sta, hop), stk),
            device_id_type=MESH,
        )

    copies = {d: link(d, parent, hop) for d, parent, hop in plan}
    children = {}
    for d, parent, _ in plan:
        children.setdefault(parent, []).append(d)
    for d in sorted(children[0], reverse=True):
        copies[d].start()

    own_ref[stk] = slots[0]
    own_copies = []
    for other in range(1, n_stk):
        peer = (sta, jnp.bitwise_xor(stk, other))
        copy = pltpu.make_async_remote_copy(
            src_ref=slots.at[0],
            dst_ref=own_ref.at[stk],
            send_sem=own_send.at[other],
            recv_sem=own_recv.at[other],
            device_id=peer,
            device_id_type=MESH,
        )
        copy.start()
        own_copies.append(copy)

    for load in loads[1:]:
        load.wait()
    first_out[...] = first_here[...].astype(jnp.bfloat16)
    last_out[...] = last_here[...].astype(jnp.bfloat16)

    for d, _, _ in plan:
        copies[d].wait_recv()
        for child in children.get(d, []):
            copies[child].start()

    far_copies = []
    for r in range(far_ref.shape[1]):
        far_ref[stk, r] = slots[masks[r]]
        for other in range(1, n_stk):
            copy = pltpu.make_async_remote_copy(
                src_ref=far_ref.at[stk, r],
                dst_ref=far_ref.at[stk, r],
                send_sem=far_send.at[r, other],
                recv_sem=far_recv.at[r, other],
                device_id=(sta, jnp.bitwise_xor(stk, other)),
                device_id_type=MESH,
            )
            copy.start()
            far_copies.append(copy)
    for d, _, _ in plan:
        copies[d].wait_send()
    for copy in own_copies + far_copies:
        copy.wait()


def split(value):
    high = value.astype(jnp.bfloat16)
    low = (value - high.astype(jnp.float32)).astype(jnp.bfloat16)
    return high, low


def transform_kernel(
    n_stk, own_ref, far_ref, first_ref, twist_ref, last_ref, out_ref, joined, turned, lagged
):
    stk = lax.axis_index("stk")
    pairs, rounds, lags = out_ref.shape
    stations = far_ref.shape[2]
    grid = far_ref.shape[4:]
    rows = grid[0]
    bin_index = LANES * lax.broadcasted_iota(jnp.int32, grid, 0) + lax.broadcasted_iota(
        jnp.int32, grid, 1
    )
    weight = jnp.where(bin_index == 0, 0.5, 1.0).astype(jnp.float32)
    lane = lax.broadcasted_iota(jnp.int32, (GROUP_ROWS, LANES), 1)
    for p in range(pairs):
        pair = stk * pairs + p
        i = pair // stations
        j = lax.rem(pair, stations)
        own = [
            [own_ref[w, i, c].astype(jnp.float32) * weight for c in range(2)]
            for w in range(n_stk)
        ]
        for r in range(rounds):
            re = im = None
            for w in range(n_stk):
                ar, ai = own[w]
                br = far_ref[w, r, j, 0].astype(jnp.float32)
                bi = far_ref[w, r, j, 1].astype(jnp.float32)
                re_w = ar * br + ai * bi
                im_w = ai * br - ar * bi
                re = re_w if re is None else re + re_w
                im = im_w if im is None else im + im_w
            re_high, re_low = split(re)
            im_high, im_low = split(im)
            parts = (re_high, im_high, re_low, im_low, re_high, im_high)
            for index, part in enumerate(parts):
                joined[
                    p, index * rows : (index + 1) * rows, r * LANES : (r + 1) * LANES
                ] = part
    for p in range(pairs):
        inner = jnp.dot(first_ref[...], joined[p], preferred_element_type=jnp.float32)
        for r in range(rounds):
            in_re = inner[:FINE, r * LANES : (r + 1) * LANES]
            in_im = inner[FINE:, r * LANES : (r + 1) * LANES]
            here = slice(r * FINE, (r + 1) * FINE)
            for c, value in enumerate(
                (
                    in_re * twist_ref[0] - in_im * twist_ref[1],
                    in_re * twist_ref[1] + in_im * twist_ref[0],
                )
            ):
                turned[p, here, c * LANES : (c + 1) * LANES] = value.astype(jnp.bfloat16)
    contract = (((1,), (1,)), ((), ()))
    for p in range(pairs):
        both = lax.dot_general(
            last_ref[...], turned[p], contract, preferred_element_type=jnp.float32
        )
        series = both[: 2 * GROUP_ROWS] + both[2 * GROUP_ROWS :]
        for half in range(rounds // 2):
            even = series[:GROUP_ROWS, half * LANES : (half + 1) * LANES]
            odd = series[GROUP_ROWS:, half * LANES : (half + 1) * LANES]
            base = (p * rounds + 2 * half) * GROUP_ROWS
            lagged[base : base + GROUP_ROWS] = jnp.where(lane < FINE, even, pltpu.roll(odd, FINE, 1))
            lagged[base + GROUP_ROWS : base + 2 * GROUP_ROWS] = jnp.where(
                lane < FINE, pltpu.roll(even, FINE, 1), odd
            )
    for p in range(pairs):
        for g in range(GROUPS):
            span = min(LANES, lags - g * LANES)
            values = lagged[pl.ds(p * rounds * GROUP_ROWS + g, rounds, stride=GROUP_ROWS), :]
            out_ref[p, :, g * LANES : g * LANES + span] = values[:, :span]


def turn(product):
    return np.remainder(product, NFFT) * (2.0 * math.pi / NFFT)


def tables(bins, windows):
    a = np.arange(bins // LANES)
    f = np.arange(FINE)
    c = np.arange(LANES)
    scale = 2.0 / math.sqrt(windows * bins)
    angle = turn(LANES * a[None, :] * (f[:, None] - MAXLAG))
    cos, sin = np.cos(angle), np.sin(angle)
    first = np.block([[cos, -sin], [sin, cos]]).astype(np.float32)
    angle = turn(c[None, :] * (f[:, None] - MAXLAG))
    twist = (np.stack([np.cos(angle), np.sin(angle)]) * scale).astype(np.float32)
    group = np.zeros((2, GROUP_ROWS), np.int64)
    group[0, :GROUPS] = 2 * np.arange(GROUPS)
    group[1, :GROUPS] = 2 * np.arange(GROUPS) + 1
    angle = turn(FINE * group.reshape(-1)[:, None] * c[None, :])
    last = np.concatenate([np.cos(angle), -np.sin(angle)], axis=1).astype(np.float32)

    def halves(table):
        high = table.astype(ml_dtypes.bfloat16).astype(np.float32)
        return high, (table - high).astype(ml_dtypes.bfloat16).astype(np.float32)

    first_high, first_low = halves(first)
    last_high, last_low = halves(last)
    return (
        np.concatenate([first_high, first_high, first_low], axis=1),
        twist,
        np.concatenate([last_high, last_low], axis=0),
    )


def body(n_sta, n_stk, spectra, partner_masks):
    _, stations, parts, bins = spectra.shape
    rounds = partner_masks.shape[0]
    rows = bins // LANES
    block = (stations, parts, rows, LANES)
    fixed = tables(bins, n_stk)
    first_shape, twist_shape, last_shape = [table.shape for table in fixed]
    operands = [
        pltpu.with_memory_space_constraint(jnp.asarray(operand), pltpu.HBM)
        for operand in (spectra, partner_masks, *fixed)
    ]
    own, far, first, twist, last = pl.pallas_call(
        functools.partial(gather_kernel, n_sta, n_stk),
        out_shape=[
            jax.ShapeDtypeStruct((n_stk,) + block, jnp.bfloat16),
            jax.ShapeDtypeStruct((n_stk, rounds) + block, jnp.bfloat16),
            jax.ShapeDtypeStruct(first_shape, jnp.bfloat16),
            jax.ShapeDtypeStruct(twist_shape, jnp.float32),
            jax.ShapeDtypeStruct(last_shape, jnp.bfloat16),
        ],
        in_specs=[pl.BlockSpec(memory_space=pltpu.HBM)] * 5,
        out_specs=[VMEM] * 5,
        scratch_shapes=[
            pltpu.VMEM(spectra.shape, jnp.float32),
            pltpu.SMEM((rounds,), jnp.int32),
            pltpu.VMEM(first_shape, jnp.float32),
            pltpu.VMEM(last_shape, jnp.float32),
            pltpu.VMEM(block, jnp.float32),
            pltpu.VMEM((n_sta,) + block, jnp.bfloat16),
            pltpu.SemaphoreType.DMA((5,)),
            pltpu.SemaphoreType.DMA((n_sta,)),
            pltpu.SemaphoreType.DMA((n_sta,)),
            pltpu.SemaphoreType.DMA((n_stk,)),
            pltpu.SemaphoreType.DMA((n_stk,)),
            pltpu.SemaphoreType.DMA((rounds, n_stk)),
            pltpu.SemaphoreType.DMA((rounds, n_stk)),
        ],
        compiler_params=pltpu.CompilerParams(
            collective_id=0, has_side_effects=True, vmem_limit_bytes=32 * 2**20
        ),
        name="whiten_gather",
    )(*operands)
    pairs = stations * stations // n_stk
    return pl.pallas_call(
        functools.partial(transform_kernel, n_stk),
        out_shape=jax.ShapeDtypeStruct((pairs, rounds, 2 * MAXLAG), jnp.float32),
        in_specs=[VMEM] * 5,
        out_specs=VMEM,
        scratch_shapes=[
            pltpu.VMEM((pairs, 6 * rows, rounds * LANES), jnp.bfloat16),
            pltpu.VMEM((pairs, rounds * FINE, 2 * LANES), jnp.bfloat16),
            pltpu.VMEM((pairs * rounds * GROUP_ROWS, LANES), jnp.float32),
        ],
        compiler_params=pltpu.CompilerParams(vmem_limit_bytes=32 * 2**20),
        name="cross_transform",
    )(own, far, first, twist, last)


def solution(mesh):
    return jax.shard_map(
        functools.partial(body, mesh.shape["sta"], mesh.shape["stk"]),
        mesh=mesh,
        in_specs=(P("stk", "sta", None, None), P()),
        out_specs=P(("sta", "stk"), None, None),
        check_vma=False,
    )
```

```python
import functools
import math

import jax
import jax.numpy as jnp
import ml_dtypes
import numpy as np
from jax import lax
from jax.experimental import pallas as pl
from jax.experimental.pallas import tpu as pltpu
from jax.sharding import PartitionSpec as P

NFFT = 8192
MAXLAG = 1200
LANES = 128
FINE = NFFT // LANES
GROUPS = -(-2 * MAXLAG // LANES)
GROUP_ROWS = -(-GROUPS // 8) * 8
MESH = pl.DeviceIdType.MESH
VMEM = pl.BlockSpec(memory_space=pltpu.VMEM)


def routes(count):
    plan = [(high, 0, high) for high in range(8, count, 4)]
    plan += [(low, 0, low) for low in (1, 2, 3)]
    plan += [(high | low, high, low) for high in range(8, count, 4) for low in (1, 2, 3)]
    plan += [(4, 0, 4)] + [(4 | low, low, 4) for low in (1, 2, 3)]
    return plan


def gather_kernel(
    n_sta, n_stk, x_ref, mask_ref, first_ref, twist_ref, last_ref,
    own_ref, far_ref, first_out, twist_out, last_out,
    x_here, masks, first_here, last_here, stage, slots, load_sem,
    send_sem, recv_sem, own_send, own_recv, far_send, far_recv,
):
    sta = lax.axis_index("sta")
    stk = lax.axis_index("stk")
    plan = routes(n_sta)
    hops = sorted({hop for _, _, hop in plan})
    sources = (x_ref, mask_ref, first_ref, twist_ref, last_ref)
    targets = (x_here, masks, first_here, twist_out, last_here)
    loads = [
        pltpu.make_async_copy(source, target, load_sem.at[index])
        for index, (source, target) in enumerate(zip(sources, targets))
    ]
    for load in loads:
        load.start()
    barrier = pltpu.get_barrier_semaphore()
    for hop in hops:
        pl.semaphore_signal(
            barrier, inc=1, device_id=(jnp.bitwise_xor(sta, hop), stk), device_id_type=MESH
        )
    for other in range(1, n_stk):
        pl.semaphore_signal(
            barrier, inc=1, device_id=(sta, jnp.bitwise_xor(stk, other)), device_id_type=MESH
        )

    loads[0].wait()
    _, stations, _, bins = x_here.shape
    rows = bins // LANES
    for s in range(stations):
        for a in range(rows):
            stage[s, :, a, :] = x_here[0, s, :, a * LANES : (a + 1) * LANES]
    for s in range(stations):
        re = stage[s, 0]
        im = stage[s, 1]
        power = re * re + im * im
        level = jnp.sum(power, keepdims=True) * (1.0 / bins)
        denom = jnp.sqrt(power + 0.05 * (level + 1e-06))
        slots[0, s, 0] = (re / denom).astype(jnp.bfloat16)
        slots[0, s, 1] = (im / denom).astype(jnp.bfloat16)

    pl.semaphore_wait(barrier, len(hops) + n_stk - 1)

    def link(d, parent, hop):
        return pltpu.make_async_remote_copy(
            src_ref=slots.at[parent],
            dst_ref=slots.at[d],
            send_sem=send_sem.at[d],
            recv_sem=recv_sem.at[d],
            device_id=(jnp.bitwise_xor(sta, hop), stk),
            device_id_type=MESH,
        )

    copies = {d: link(d, parent, hop) for d, parent, hop in plan}
    children = {}
    for d, parent, _ in plan:
        children.setdefault(parent, []).append(d)
    for d in sorted(children[0], reverse=True):
        copies[d].start()

    own_ref[stk] = slots[0]
    own_copies = []
    for other in range(1, n_stk):
        peer = (sta, jnp.bitwise_xor(stk, other))
        copy = pltpu.make_async_remote_copy(
            src_ref=slots.at[0],
            dst_ref=own_ref.at[stk],
            send_sem=own_send.at[other],
            recv_sem=own_recv.at[other],
            device_id=peer,
            device_id_type=MESH,
        )
        copy.start()
        own_copies.append(copy)

    for d, _, _ in plan:
        copies[d].wait_recv()
        for child in children.get(d, []):
            copies[child].start()

    loads[1].wait()
    far_copies = []
    for r in range(far_ref.shape[1]):
        far_ref[stk, r] = slots[masks[r]]
        for other in range(1, n_stk):
            copy = pltpu.make_async_remote_copy(
                src_ref=far_ref.at[stk, r],
                dst_ref=far_ref.at[stk, r],
                send_sem=far_send.at[r, other],
                recv_sem=far_recv.at[r, other],
                device_id=(sta, jnp.bitwise_xor(stk, other)),
                device_id_type=MESH,
            )
            copy.start()
            far_copies.append(copy)
    for load in loads[2:]:
        load.wait()
    first_out[...] = first_here[...].astype(jnp.bfloat16)
    last_out[...] = last_here[...].astype(jnp.bfloat16)
    for d, _, _ in plan:
        copies[d].wait_send()
    for copy in own_copies + far_copies:
        copy.wait()


def split(value):
    high = value.astype(jnp.bfloat16)
    low = (value - high.astype(jnp.float32)).astype(jnp.bfloat16)
    return high, low


def transform_kernel(
    n_stk, own_ref, far_ref, first_ref, twist_ref, last_ref, out_ref, joined, turned, lagged
):
    stk = lax.axis_index("stk")
    pairs, rounds, lags = out_ref.shape
    stations = far_ref.shape[2]
    grid = far_ref.shape[4:]
    rows = grid[0]
    bin_index = LANES * lax.broadcasted_iota(jnp.int32, grid, 0) + lax.broadcasted_iota(
        jnp.int32, grid, 1
    )
    weight = jnp.where(bin_index == 0, 0.5, 1.0).astype(jnp.float32)
    lane = lax.broadcasted_iota(jnp.int32, (GROUP_ROWS, LANES), 1)
    for p in range(pairs):
        pair = stk * pairs + p
        i = pair // stations
        j = lax.rem(pair, stations)
        own = [
            [own_ref[w, i, c].astype(jnp.float32) * weight for c in range(2)]
            for w in range(n_stk)
        ]
        for r in range(rounds):
            re = im = None
            for w in range(n_stk):
                ar, ai = own[w]
                br = far_ref[w, r, j, 0].astype(jnp.float32)
                bi = far_ref[w, r, j, 1].astype(jnp.float32)
                re_w = ar * br + ai * bi
                im_w = ai * br - ar * bi
                re = re_w if re is None else re + re_w
                im = im_w if im is None else im + im_w
            re_high, re_low = split(re)
            im_high, im_low = split(im)
            parts = (re_high, im_high, re_low, im_low, re_high, im_high)
            for index, part in enumerate(parts):
                joined[
                    p, index * rows : (index + 1) * rows, r * LANES : (r + 1) * LANES
                ] = part
    for p in range(pairs):
        inner = jnp.dot(first_ref[...], joined[p], preferred_element_type=jnp.float32)
        for r in range(rounds):
            in_re = inner[:FINE, r * LANES : (r + 1) * LANES]
            in_im = inner[FINE:, r * LANES : (r + 1) * LANES]
            here = slice(r * FINE, (r + 1) * FINE)
            for c, value in enumerate(
                (
                    in_re * twist_ref[0] - in_im * twist_ref[1],
                    in_re * twist_ref[1] + in_im * twist_ref[0],
                )
            ):
                turned[p, here, c * LANES : (c + 1) * LANES] = value.astype(jnp.bfloat16)
    contract = (((1,), (1,)), ((), ()))
    for p in range(pairs):
        both = lax.dot_general(
            last_ref[...], turned[p], contract, preferred_element_type=jnp.float32
        )
        series = both[: 2 * GROUP_ROWS] + both[2 * GROUP_ROWS :]
        for half in range(rounds // 2):
            even = series[:GROUP_ROWS, half * LANES : (half + 1) * LANES]
            odd = series[GROUP_ROWS:, half * LANES : (half + 1) * LANES]
            base = (p * rounds + 2 * half) * GROUP_ROWS
            lagged[base : base + GROUP_ROWS] = jnp.where(lane < FINE, even, pltpu.roll(odd, FINE, 1))
            lagged[base + GROUP_ROWS : base + 2 * GROUP_ROWS] = jnp.where(
                lane < FINE, pltpu.roll(even, FINE, 1), odd
            )
    for p in range(pairs):
        for g in range(GROUPS):
            span = min(LANES, lags - g * LANES)
            values = lagged[pl.ds(p * rounds * GROUP_ROWS + g, rounds, stride=GROUP_ROWS), :]
            out_ref[p, :, g * LANES : g * LANES + span] = values[:, :span]


def turn(product):
    return np.remainder(product, NFFT) * (2.0 * math.pi / NFFT)


def tables(bins, windows):
    a = np.arange(bins // LANES)
    f = np.arange(FINE)
    c = np.arange(LANES)
    scale = 2.0 / math.sqrt(windows * bins)
    angle = turn(LANES * a[None, :] * (f[:, None] - MAXLAG))
    cos, sin = np.cos(angle), np.sin(angle)
    first = np.block([[cos, -sin], [sin, cos]]).astype(np.float32)
    angle = turn(c[None, :] * (f[:, None] - MAXLAG))
    twist = (np.stack([np.cos(angle), np.sin(angle)]) * scale).astype(np.float32)
    group = np.zeros((2, GROUP_ROWS), np.int64)
    group[0, :GROUPS] = 2 * np.arange(GROUPS)
    group[1, :GROUPS] = 2 * np.arange(GROUPS) + 1
    angle = turn(FINE * group.reshape(-1)[:, None] * c[None, :])
    last = np.concatenate([np.cos(angle), -np.sin(angle)], axis=1).astype(np.float32)

    def halves(table):
        high = table.astype(ml_dtypes.bfloat16).astype(np.float32)
        return high, (table - high).astype(ml_dtypes.bfloat16).astype(np.float32)

    first_high, first_low = halves(first)
    last_high, last_low = halves(last)
    return (
        np.concatenate([first_high, first_high, first_low], axis=1),
        twist,
        np.concatenate([last_high, last_low], axis=0),
    )


def body(n_sta, n_stk, spectra, partner_masks):
    _, stations, parts, bins = spectra.shape
    rounds = partner_masks.shape[0]
    rows = bins // LANES
    block = (stations, parts, rows, LANES)
    fixed = tables(bins, n_stk)
    first_shape, twist_shape, last_shape = [table.shape for table in fixed]
    operands = [
        pltpu.with_memory_space_constraint(jnp.asarray(operand), pltpu.HBM)
        for operand in (spectra, partner_masks, *fixed)
    ]
    own, far, first, twist, last = pl.pallas_call(
        functools.partial(gather_kernel, n_sta, n_stk),
        out_shape=[
            jax.ShapeDtypeStruct((n_stk,) + block, jnp.bfloat16),
            jax.ShapeDtypeStruct((n_stk, rounds) + block, jnp.bfloat16),
            jax.ShapeDtypeStruct(first_shape, jnp.bfloat16),
            jax.ShapeDtypeStruct(twist_shape, jnp.float32),
            jax.ShapeDtypeStruct(last_shape, jnp.bfloat16),
        ],
        in_specs=[pl.BlockSpec(memory_space=pltpu.HBM)] * 5,
        out_specs=[VMEM] * 5,
        scratch_shapes=[
            pltpu.VMEM(spectra.shape, jnp.float32),
            pltpu.SMEM((rounds,), jnp.int32),
            pltpu.VMEM(first_shape, jnp.float32),
            pltpu.VMEM(last_shape, jnp.float32),
            pltpu.VMEM(block, jnp.float32),
            pltpu.VMEM((n_sta,) + block, jnp.bfloat16),
            pltpu.SemaphoreType.DMA((5,)),
            pltpu.SemaphoreType.DMA((n_sta,)),
            pltpu.SemaphoreType.DMA((n_sta,)),
            pltpu.SemaphoreType.DMA((n_stk,)),
            pltpu.SemaphoreType.DMA((n_stk,)),
            pltpu.SemaphoreType.DMA((rounds, n_stk)),
            pltpu.SemaphoreType.DMA((rounds, n_stk)),
        ],
        compiler_params=pltpu.CompilerParams(
            collective_id=0, has_side_effects=True, vmem_limit_bytes=32 * 2**20
        ),
        name="whiten_gather",
    )(*operands)
    pairs = stations * stations // n_stk
    return pl.pallas_call(
        functools.partial(transform_kernel, n_stk),
        out_shape=jax.ShapeDtypeStruct((pairs, rounds, 2 * MAXLAG), jnp.float32),
        in_specs=[VMEM] * 5,
        out_specs=VMEM,
        scratch_shapes=[
            pltpu.VMEM((pairs, 6 * rows, rounds * LANES), jnp.bfloat16),
            pltpu.VMEM((pairs, rounds * FINE, 2 * LANES), jnp.bfloat16),
            pltpu.VMEM((pairs * rounds * GROUP_ROWS, LANES), jnp.float32),
        ],
        compiler_params=pltpu.CompilerParams(vmem_limit_bytes=32 * 2**20),
        name="cross_transform",
    )(own, far, first, twist, last)


def solution(mesh):
    return jax.shard_map(
        functools.partial(body, mesh.shape["sta"], mesh.shape["stk"]),
        mesh=mesh,
        in_specs=(P("stk", "sta", None, None), P()),
        out_specs=P(("sta", "stk"), None, None),
        check_vma=False,
    )
```

```python
import functools
import math

import jax
import jax.numpy as jnp
import ml_dtypes
import numpy as np
from jax import lax
from jax.experimental import pallas as pl
from jax.experimental.pallas import tpu as pltpu
from jax.sharding import PartitionSpec as P

NFFT = 8192
MAXLAG = 1200
LANES = 128
FINE = NFFT // LANES
GROUPS = -(-2 * MAXLAG // LANES)
GROUP_ROWS = -(-GROUPS // 8) * 8
MESH = pl.DeviceIdType.MESH
VMEM = pl.BlockSpec(memory_space=pltpu.VMEM)


def routes(count):
    plan = [(high, 0, high) for high in reversed(range(4, count, 4))]
    plan += [(low, 0, low) for low in (3, 1, 2)]
    plan += [(high | low, high, low) for high in range(8, count, 4) for low in (3, 1, 2)]
    plan += [(4 | low, low, 4) for low in (1, 2, 3)]
    return plan


def gather_kernel(
    n_sta, n_stk, x_ref, mask_ref, first_ref, twist_ref, last_ref,
    own_ref, far_ref, first_out, twist_out, last_out,
    x_here, masks, first_here, last_here, stage, slots, load_sem,
    send_sem, recv_sem, own_send, own_recv, far_send, far_recv,
):
    sta = lax.axis_index("sta")
    stk = lax.axis_index("stk")
    plan = routes(n_sta)
    hops = sorted({hop for _, _, hop in plan})
    sources = (x_ref, mask_ref, first_ref, twist_ref, last_ref)
    targets = (x_here, masks, first_here, twist_out, last_here)
    loads = [
        pltpu.make_async_copy(source, target, load_sem.at[index])
        for index, (source, target) in enumerate(zip(sources, targets))
    ]
    for load in loads:
        load.start()
    barrier = pltpu.get_barrier_semaphore()
    for hop in hops:
        pl.semaphore_signal(
            barrier, inc=1, device_id=(jnp.bitwise_xor(sta, hop), stk), device_id_type=MESH
        )
    for other in range(1, n_stk):
        pl.semaphore_signal(
            barrier, inc=1, device_id=(sta, jnp.bitwise_xor(stk, other)), device_id_type=MESH
        )

    loads[0].wait()
    _, stations, _, bins = x_here.shape
    rows = bins // LANES
    for s in range(stations):
        for a in range(rows):
            stage[s, :, a, :] = x_here[0, s, :, a * LANES : (a + 1) * LANES]
    for s in range(stations):
        re = stage[s, 0]
        im = stage[s, 1]
        power = re * re + im * im
        level = jnp.sum(power, keepdims=True) * (1.0 / bins)
        denom = jnp.sqrt(power + 0.05 * (level + 1e-06))
        slots[0, s, 0] = (re / denom).astype(jnp.bfloat16)
        slots[0, s, 1] = (im / denom).astype(jnp.bfloat16)

    pl.semaphore_wait(barrier, len(hops) + n_stk - 1)

    def link(d, parent, hop):
        return pltpu.make_async_remote_copy(
            src_ref=slots.at[parent],
            dst_ref=slots.at[d],
            send_sem=send_sem.at[d],
            recv_sem=recv_sem.at[d],
            device_id=(jnp.bitwise_xor(sta, hop), stk),
            device_id_type=MESH,
        )

    copies = {d: link(d, parent, hop) for d, parent, hop in plan}
    children = {}
    for d, parent, _ in plan:
        children.setdefault(parent, []).append(d)
    for d in children[0]:
        copies[d].start()

    own_ref[stk] = slots[0]
    own_copies = []
    for other in range(1, n_stk):
        peer = (sta, jnp.bitwise_xor(stk, other))
        copy = pltpu.make_async_remote_copy(
            src_ref=slots.at[0],
            dst_ref=own_ref.at[stk],
            send_sem=own_send.at[other],
            recv_sem=own_recv.at[other],
            device_id=peer,
            device_id_type=MESH,
        )
        copy.start()
        own_copies.append(copy)

    for load in loads[1:]:
        load.wait()
    first_out[...] = first_here[...].astype(jnp.bfloat16)
    last_out[...] = last_here[...].astype(jnp.bfloat16)

    for d, _, _ in plan:
        copies[d].wait_recv()
        for child in children.get(d, []):
            copies[child].start()

    far_copies = []
    for r in range(far_ref.shape[1]):
        far_ref[stk, r] = slots[masks[r]]
        for other in range(1, n_stk):
            copy = pltpu.make_async_remote_copy(
                src_ref=far_ref.at[stk, r],
                dst_ref=far_ref.at[stk, r],
                send_sem=far_send.at[r, other],
                recv_sem=far_recv.at[r, other],
                device_id=(sta, jnp.bitwise_xor(stk, other)),
                device_id_type=MESH,
            )
            copy.start()
            far_copies.append(copy)
    for d, _, _ in plan:
        copies[d].wait_send()
    for copy in own_copies + far_copies:
        copy.wait()


def split(value):
    high = value.astype(jnp.bfloat16)
    low = (value - high.astype(jnp.float32)).astype(jnp.bfloat16)
    return high, low


def transform_kernel(
    n_stk, own_ref, far_ref, first_ref, twist_ref, last_ref, out_ref, joined, turned, lagged
):
    stk = lax.axis_index("stk")
    pairs, rounds, lags = out_ref.shape
    stations = far_ref.shape[2]
    grid = far_ref.shape[4:]
    rows = grid[0]
    bin_index = LANES * lax.broadcasted_iota(jnp.int32, grid, 0) + lax.broadcasted_iota(
        jnp.int32, grid, 1
    )
    weight = jnp.where(bin_index == 0, 0.5, 1.0).astype(jnp.float32)
    lane = lax.broadcasted_iota(jnp.int32, (GROUP_ROWS, LANES), 1)
    for p in range(pairs):
        pair = stk * pairs + p
        i = pair // stations
        j = lax.rem(pair, stations)
        own = [
            [own_ref[w, i, c].astype(jnp.float32) * weight for c in range(2)]
            for w in range(n_stk)
        ]
        for r in range(rounds):
            re = im = None
            for w in range(n_stk):
                ar, ai = own[w]
                br = far_ref[w, r, j, 0].astype(jnp.float32)
                bi = far_ref[w, r, j, 1].astype(jnp.float32)
                re_w = ar * br + ai * bi
                im_w = ai * br - ar * bi
                re = re_w if re is None else re + re_w
                im = im_w if im is None else im + im_w
            re_high, re_low = split(re)
            im_high, im_low = split(im)
            parts = (re_high, im_high, re_low, im_low, re_high, im_high)
            for index, part in enumerate(parts):
                joined[
                    p, index * rows : (index + 1) * rows, r * LANES : (r + 1) * LANES
                ] = part
    for p in range(pairs):
        inner = jnp.dot(first_ref[...], joined[p], preferred_element_type=jnp.float32)
        for r in range(rounds):
            in_re = inner[:FINE, r * LANES : (r + 1) * LANES]
            in_im = inner[FINE:, r * LANES : (r + 1) * LANES]
            here = slice(r * FINE, (r + 1) * FINE)
            for c, value in enumerate(
                (
                    in_re * twist_ref[0] - in_im * twist_ref[1],
                    in_re * twist_ref[1] + in_im * twist_ref[0],
                )
            ):
                turned[p, here, c * LANES : (c + 1) * LANES] = value.astype(jnp.bfloat16)
    contract = (((1,), (1,)), ((), ()))
    for p in range(pairs):
        both = lax.dot_general(
            last_ref[...], turned[p], contract, preferred_element_type=jnp.float32
        )
        series = both[: 2 * GROUP_ROWS] + both[2 * GROUP_ROWS :]
        for half in range(rounds // 2):
            even = series[:GROUP_ROWS, half * LANES : (half + 1) * LANES]
            odd = series[GROUP_ROWS:, half * LANES : (half + 1) * LANES]
            base = (p * rounds + 2 * half) * GROUP_ROWS
            lagged[base : base + GROUP_ROWS] = jnp.where(lane < FINE, even, pltpu.roll(odd, FINE, 1))
            lagged[base + GROUP_ROWS : base + 2 * GROUP_ROWS] = jnp.where(
                lane < FINE, pltpu.roll(even, FINE, 1), odd
            )
    for p in range(pairs):
        for g in range(GROUPS):
            span = min(LANES, lags - g * LANES)
            values = lagged[pl.ds(p * rounds * GROUP_ROWS + g, rounds, stride=GROUP_ROWS), :]
            out_ref[p, :, g * LANES : g * LANES + span] = values[:, :span]


def turn(product):
    return np.remainder(product, NFFT) * (2.0 * math.pi / NFFT)


def tables(bins, windows):
    a = np.arange(bins // LANES)
    f = np.arange(FINE)
    c = np.arange(LANES)
    scale = 2.0 / math.sqrt(windows * bins)
    angle = turn(LANES * a[None, :] * (f[:, None] - MAXLAG))
    cos, sin = np.cos(angle), np.sin(angle)
    first = np.block([[cos, -sin], [sin, cos]]).astype(np.float32)
    angle = turn(c[None, :] * (f[:, None] - MAXLAG))
    twist = (np.stack([np.cos(angle), np.sin(angle)]) * scale).astype(np.float32)
    group = np.zeros((2, GROUP_ROWS), np.int64)
    group[0, :GROUPS] = 2 * np.arange(GROUPS)
    group[1, :GROUPS] = 2 * np.arange(GROUPS) + 1
    angle = turn(FINE * group.reshape(-1)[:, None] * c[None, :])
    last = np.concatenate([np.cos(angle), -np.sin(angle)], axis=1).astype(np.float32)

    def halves(table):
        high = table.astype(ml_dtypes.bfloat16).astype(np.float32)
        return high, (table - high).astype(ml_dtypes.bfloat16).astype(np.float32)

    first_high, first_low = halves(first)
    last_high, last_low = halves(last)
    return (
        np.concatenate([first_high, first_high, first_low], axis=1),
        twist,
        np.concatenate([last_high, last_low], axis=0),
    )


def body(n_sta, n_stk, spectra, partner_masks):
    _, stations, parts, bins = spectra.shape
    rounds = partner_masks.shape[0]
    rows = bins // LANES
    block = (stations, parts, rows, LANES)
    fixed = tables(bins, n_stk)
    first_shape, twist_shape, last_shape = [table.shape for table in fixed]
    operands = [
        pltpu.with_memory_space_constraint(jnp.asarray(operand), pltpu.HBM)
        for operand in (spectra, partner_masks, *fixed)
    ]
    own, far, first, twist, last = pl.pallas_call(
        functools.partial(gather_kernel, n_sta, n_stk),
        out_shape=[
            jax.ShapeDtypeStruct((n_stk,) + block, jnp.bfloat16),
            jax.ShapeDtypeStruct((n_stk, rounds) + block, jnp.bfloat16),
            jax.ShapeDtypeStruct(first_shape, jnp.bfloat16),
            jax.ShapeDtypeStruct(twist_shape, jnp.float32),
            jax.ShapeDtypeStruct(last_shape, jnp.bfloat16),
        ],
        in_specs=[pl.BlockSpec(memory_space=pltpu.HBM)] * 5,
        out_specs=[VMEM] * 5,
        scratch_shapes=[
            pltpu.VMEM(spectra.shape, jnp.float32),
            pltpu.SMEM((rounds,), jnp.int32),
            pltpu.VMEM(first_shape, jnp.float32),
            pltpu.VMEM(last_shape, jnp.float32),
            pltpu.VMEM(block, jnp.float32),
            pltpu.VMEM((n_sta,) + block, jnp.bfloat16),
            pltpu.SemaphoreType.DMA((5,)),
            pltpu.SemaphoreType.DMA((n_sta,)),
            pltpu.SemaphoreType.DMA((n_sta,)),
            pltpu.SemaphoreType.DMA((n_stk,)),
            pltpu.SemaphoreType.DMA((n_stk,)),
            pltpu.SemaphoreType.DMA((rounds, n_stk)),
            pltpu.SemaphoreType.DMA((rounds, n_stk)),
        ],
        compiler_params=pltpu.CompilerParams(
            collective_id=0, has_side_effects=True, vmem_limit_bytes=32 * 2**20
        ),
        name="whiten_gather",
    )(*operands)
    pairs = stations * stations // n_stk
    return pl.pallas_call(
        functools.partial(transform_kernel, n_stk),
        out_shape=jax.ShapeDtypeStruct((pairs, rounds, 2 * MAXLAG), jnp.float32),
        in_specs=[VMEM] * 5,
        out_specs=VMEM,
        scratch_shapes=[
            pltpu.VMEM((pairs, 6 * rows, rounds * LANES), jnp.bfloat16),
            pltpu.VMEM((pairs, rounds * FINE, 2 * LANES), jnp.bfloat16),
            pltpu.VMEM((pairs * rounds * GROUP_ROWS, LANES), jnp.float32),
        ],
        compiler_params=pltpu.CompilerParams(vmem_limit_bytes=32 * 2**20),
        name="cross_transform",
    )(own, far, first, twist, last)


def solution(mesh):
    return jax.shard_map(
        functools.partial(body, mesh.shape["sta"], mesh.shape["stk"]),
        mesh=mesh,
        in_specs=(P("stk", "sta", None, None), P()),
        out_specs=P(("sta", "stk"), None, None),
        check_vma=False,
    )
```
